128 devices in a mesh: prefix: 16 (over z, y), group: 8 (over x, core).
Axes of the slice: x: 4, y: 4, z: 4, core: 2. Of those that a mesh axis runs over, the one named last changes fastest.
Arguments:
- queries: bfloat16 [16, 256, 8192], P(None, 'group', 'prefix'), may hold values from -128 to 128
- cand_kv: bfloat16 [16, 256, 2048], P(None, 'group'), may hold values from -32 to 32
- prefix_kv: bfloat16 [16384, 2048], P('prefix'), may hold values from -32 to 32
- lengths: int32 [16], replicated, may hold values from 32 to 256, as said below
- owner: int32 [16], replicated, may hold values from 0 to 7, as said below
Outputs:
- scored: bfloat16 [16, 256, 8192], P('group', None, 'prefix')
The draws below stay inside these ranges and needn't reach their ends.
Inputs may be any that keep to these rules, and one draw needn't show every extreme that they name: Passage lengths; some passage has exactly 256 tokens in every draw. Every group number is the owner of exactly 2 passages.
All inputs are finite; a program needn't handle non-finite values.
Results may differ from the reference program's by a relative error of at most 0.0095.
Values may be sent and summed in bfloat16 or wider, within the bound.
No kernel may reach another device: no remote copies, remote signals or barrier semaphores. Data moves between devices by JAX's collectives and lax.ppermute only.
A program may use at most 192 MiB of HBM per device.

```python
import math
import jax
import jax.numpy as jnp
from jax import lax

H = 64
KVH = 8
HD = 128
PREFIX = 16384
PLEN = 256
PASS_GROUP = 2
PASSAGES = 16


def anchor_rows(key):
    return jnp.clip(jax.random.normal(key, (KVH, HD), jnp.float32), -4.0, 4.0)


def draw_queries(key, part):
    key = jax.random.fold_in(key, 11)
    base = jnp.clip(2.0 * jax.random.normal(key, (PASSAGES, PLEN, H * HD), jnp.float32), -12.0, 12.0)
    return base.astype(jnp.bfloat16)


def draw_prefix_kv(key, part):
    anchor = anchor_rows(key)
    key = jax.random.fold_in(key, 12)
    key_part, value_part = jax.random.split(key)
    ramp = 0.7 + 0.6 * jnp.arange(PREFIX, dtype=jnp.float32) / PREFIX
    keys = jnp.clip(jax.random.normal(key_part, (PREFIX, KVH * HD), jnp.float32), -4.0, 4.0) * ramp[:, None]
    flat_anchor = anchor.reshape(KVH * HD)
    keys = keys.at[PREFIX // 2 + 5].set(flat_anchor)
    keys = keys.at[PREFIX - 3].set(flat_anchor * 0.991)
    values = jnp.clip(jax.random.normal(value_part, (PREFIX, KVH * HD), jnp.float32), -4.0, 4.0)
    return jnp.concatenate([keys, values], axis=1).astype(jnp.bfloat16)


def draw_cand_kv(key, part):
    key = jax.random.fold_in(key, 13)
    key_part, value_part = jax.random.split(key)
    keys = 1.5 * jnp.clip(jax.random.normal(key_part, (PASSAGES, PLEN, KVH * HD), jnp.float32), -4.0, 4.0)
    values = jnp.clip(jax.random.normal(value_part, (PASSAGES, PLEN, KVH * HD), jnp.float32), -4.0, 4.0)
    return jnp.concatenate([keys, values], axis=2).astype(jnp.bfloat16)


def draw_lengths(key, part):
    key = jax.random.fold_in(key, 14)
    first, second = jax.random.split(key)
    drawn = jax.random.randint(first, (PASSAGES,), PLEN // 8, PLEN + 1, jnp.int32)
    longest = jax.random.randint(second, (), 0, PASSAGES, jnp.int32)
    return drawn.at[longest].set(PLEN)


def draw_owner(key, part):
    key = jax.random.fold_in(key, 15)
    shuffled = jax.random.permutation(key, PASSAGES).astype(jnp.int32)
    return shuffled // PASS_GROUP


def setup_inputs(seed: int = 0) -> dict:
    arg_keys = jax.random.split(jax.random.key(seed), 6)
    queries = draw_queries(jax.random.fold_in(arg_keys[5], 71), 0)
    cand_kv = draw_cand_kv(jax.random.fold_in(arg_keys[5], 71), 0)
    prefix_kv = draw_prefix_kv(jax.random.fold_in(arg_keys[5], 71), 0)
    lengths = draw_lengths(jax.random.fold_in(arg_keys[5], 71), 0)
    owner = draw_owner(jax.random.fold_in(arg_keys[5], 71), 0)
    return {"queries": queries, "cand_kv": cand_kv, "prefix_kv": prefix_kv, "lengths": lengths, "owner": owner}


def reference(queries, cand_kv, prefix_kv, lengths, owner):
    ratio = H // KVH
    inv_root = 1.0 / math.sqrt(HD)
    ranked = jnp.argsort(owner, stable=True).astype(jnp.int32)
    sorted_q = jnp.take(queries, ranked, axis=0)
    sorted_kv = jnp.take(cand_kv, ranked, axis=0)
    sorted_len = jnp.take(lengths, ranked, axis=0)
    pre_keys = prefix_kv[:, :KVH * HD].reshape(PREFIX, KVH, HD).transpose(1, 0, 2).astype(jnp.float32)
    pre_vals = prefix_kv[:, KVH * HD:].reshape(PREFIX, KVH, HD).transpose(1, 0, 2).astype(jnp.float32)
    positions = jnp.arange(PLEN, dtype=jnp.int32)

    def one_passage(inputs):
        passage_q, passage_kv, length = inputs
        query_heads = passage_q.reshape(PLEN, KVH, ratio, HD).transpose(1, 0, 2, 3).astype(jnp.float32)
        own_keys = passage_kv[:, :KVH * HD].reshape(PLEN, KVH, HD).transpose(1, 0, 2).astype(jnp.float32)
        own_vals = passage_kv[:, KVH * HD:].reshape(PLEN, KVH, HD).transpose(1, 0, 2).astype(jnp.float32)
        allowed = (positions[None, :] <= positions[:, None]) & (positions[None, :] < length)
        allowed = allowed[:, None, :]

        def one_head(head_inputs):
            head_q, head_k, head_v, self_k, self_v = head_inputs
            pre_scores = jnp.einsum('tgd,kd->tgk', head_q, head_k) * inv_root
            pre_top = lax.optimization_barrier(jnp.max(pre_scores, axis=-1))
            pre_weights = jnp.exp(pre_scores - pre_top[..., None]).astype(jnp.bfloat16)
            pre_weights = lax.optimization_barrier(pre_weights).astype(jnp.float32)
            pre_total = lax.optimization_barrier(jnp.sum(pre_weights, axis=-1))
            pre_out = jnp.einsum('tgk,kd->tgd', pre_weights, head_v)
            self_scores = jnp.einsum('tgd,sd->tgs', head_q, self_k) * inv_root
            self_top = lax.optimization_barrier(jnp.max(jnp.where(allowed, self_scores, -jnp.inf), axis=-1))
            shifted = jnp.minimum(self_scores - self_top[..., None], 0.0)
            self_weights = jnp.where(allowed, jnp.exp(shifted), 0.0).astype(jnp.bfloat16)
            self_weights = lax.optimization_barrier(self_weights).astype(jnp.float32)
            self_total = lax.optimization_barrier(jnp.sum(self_weights, axis=-1))
            self_out = jnp.einsum('tgs,sd->tgd', self_weights, self_v)
            joint = jnp.maximum(pre_top, self_top)
            pre_factor = jnp.exp(pre_top - joint)
            self_factor = jnp.exp(self_top - joint)
            numer = pre_out * pre_factor[..., None] + self_out * self_factor[..., None]
            denom = pre_total * pre_factor + self_total * self_factor
            return numer / denom[..., None]
        heads_out = lax.map(one_head, (query_heads, pre_keys, pre_vals, own_keys, own_vals))
        merged = heads_out.transpose(1, 0, 2, 3).reshape(PLEN, H * HD)
        merged = jnp.where(positions[:, None] < length, merged, 0.0)
        return merged.astype(jnp.bfloat16)
    return lax.map(one_passage, (sorted_q, sorted_kv, sorted_len))
```

```python
import functools
import math

import jax
import jax.numpy as jnp
from jax import lax
from jax.experimental import pallas as pl
from jax.experimental.pallas import tpu as pltpu
from jax.sharding import PartitionSpec as P

H = 64
KVH = 8
HD = 128
NT = (((1,), (1,)), ((), ()))
NN = (((1,), (0,)), ((), ()))
SCALE = math.log2(math.e) / math.sqrt(HD)
LOW = -1e30
VMEM = pl.BlockSpec(memory_space=pltpu.VMEM)
SMEM = pl.BlockSpec(memory_space=pltpu.SMEM)
ANY = pl.BlockSpec(memory_space=pl.ANY)
LIMIT = 56 * 2**20
TB = 32
RB = 4
KB = 512


def run_all(copies):
    for copy in copies:
        copy.start()
    for copy in copies:
        copy.wait()


def prep_kernel(info, q, cand, kv, csend, kvsend, sem):
    head = pl.multiple_of(info[0] * HD, HD)
    rows = pl.ds(pl.multiple_of(info[3] * HD, HD), HD)
    copies = [
        pltpu.make_async_copy(q, csend.at[:, :, 0:512], sem.at[0]),
        pltpu.make_async_copy(cand.at[:, :, pl.ds(head, HD)], csend.at[:, :, 512:640], sem.at[1]),
        pltpu.make_async_copy(
            cand.at[:, :, pl.ds(pl.multiple_of(head + KVH * HD, HD), HD)],
            csend.at[:, :, 640:768],
            sem.at[2],
        ),
    ]
    for dest in range(16):
        for half in range(2):
            column = (half * KVH + dest // 2) * HD
            copies.append(
                pltpu.make_async_copy(
                    kv.at[rows, column : column + HD],
                    kvsend.at[dest, :, half * HD : (half + 1) * HD],
                    sem.at[3 + dest * 2 + half],
                )
            )
    run_all(copies)


def prep(info, q, cand, kv):
    return pl.pallas_call(
        prep_kernel,
        out_shape=(
            jax.ShapeDtypeStruct((16, 32, 768), jnp.bfloat16),
            jax.ShapeDtypeStruct((16, 128, 256), jnp.bfloat16),
        ),
        in_specs=[SMEM, ANY, ANY, ANY],
        out_specs=(ANY, ANY),
        scratch_shapes=[pltpu.SemaphoreType.DMA((35,))],
        name="prep",
    )(info, q, cand, kv)


def pack_kernel(owner, info, mine, other, b0, b1, b2, b3, count, sem):
    x, core = info[1], info[2]
    bufs = (b0, b1, b2, b3)
    for o in range(8):
        count[o] = 0

    def each(act):
        for i in range(16):
            o = owner[i]
            slot = count[o]
            count[o] = slot + 1
            ox = o // 2

            @pl.when(o % 2 == core)
            def _(i=i, slot=slot, ox=ox):
                def block(src, source_core):
                    row = pl.multiple_of(ox * 128 + slot * 64 + source_core * 32, 32)
                    for b in range(4):
                        act(src.at[i, :, 0:512], bufs[b].at[pl.ds(row, 32), :], b)
                    for b in range(4):

                        @pl.when(ox == lax.rem(x + b, 4))
                        def _(b=b):
                            act(
                                src.at[i, :, 512:768],
                                bufs[b].at[
                                    pl.ds(pl.multiple_of(512 + source_core * 32, 32), 32),
                                    pl.ds(pl.multiple_of(slot * 256, 256), 256),
                                ],
                                4 + b,
                            )

                block(mine, core)
                block(other, 1 - core)

    each(lambda s, d, k: pltpu.make_async_copy(s, d, sem.at[k]).start())
    for b in range(4):
        pltpu.make_async_copy(bufs[b].at[0:512, :], bufs[b].at[0:512, :], sem.at[b]).wait()
        pltpu.make_async_copy(bufs[b].at[512:576, :], bufs[b].at[512:576, :], sem.at[4 + b]).wait()


def pack(owner, info, mine, other):
    return pl.pallas_call(
        pack_kernel,
        out_shape=(jax.ShapeDtypeStruct((576, 512), jnp.bfloat16),) * 4,
        in_specs=[SMEM, SMEM, ANY, ANY],
        out_specs=(ANY,) * 4,
        scratch_shapes=[pltpu.SMEM((8,), jnp.int32), pltpu.SemaphoreType.DMA((8,))],
        name="pack",
    )(owner, info, mine, other)


def slot_lengths(owner, lengths, group):
    first, second, seen = 0, 0, 0
    for i in range(16):
        hit = owner[i] == group
        first = jnp.where(hit & (seen == 0), lengths[i], first)
        second = jnp.where(hit & (seen == 1), lengths[i], second)
        seen = seen + hit.astype(jnp.int32)
    return first, second


def pieces(v):
    hi = v.astype(jnp.bfloat16).astype(jnp.float32)
    mid = (v - hi).astype(jnp.bfloat16).astype(jnp.float32)
    return hi, mid, v - hi - mid


def flash_kernel(shift, own, owner, lengths, info, b0, b1, b2, b3, kv0, kv1, *rest):
    if own:
        out, stats, qraw, okv, qs, v1, sem = rest
    else:
        out, qraw, qs, v1, sem = rest
    x, core = info[1], info[2]
    dest = lax.rem(x + shift, 4)
    len0, len1 = slot_lengths(owner, lengths, dest * 2 + core)
    copies = []
    for b, buf in enumerate((b0, b1, b2, b3)):
        source = lax.rem(x + 4 - b, 4)
        rows = pl.ds(pl.multiple_of(dest * 128, 128), 128)
        copies.append(pltpu.make_async_copy(buf.at[rows, :], qraw.at[source], sem.at[b]))
        if own:
            copies.append(pltpu.make_async_copy(buf.at[512:576, :], okv.at[source], sem.at[4 + b]))
    for c in copies:
        c.start()
    for half, kv in enumerate((kv0, kv1)):
        v1[half * 2048 : (half + 1) * 2048, 0:HD] = kv[:, HD : 2 * HD]
    v1[:, HD : 2 * HD] = jnp.ones((4096, HD), jnp.bfloat16)
    for c in copies:
        c.wait()
    n0 = lax.div(len0 + (TB - 1), TB)
    total = n0 + lax.div(len1 + (TB - 1), TB)

    def place(n):
        slot = (n >= n0).astype(jnp.int32)
        return slot, n - slot * n0

    @pl.loop(0, total)
    def _(n):
        slot, tb = place(n)
        rows = pl.ds(pl.multiple_of(slot * 64 + lax.rem(tb, 2) * TB, TB), TB)
        block = lax.div(n, RB)
        base = lax.rem(n, RB) * TB
        for h in range(4):
            qs[block, pl.ds(pl.multiple_of(h * RB * TB + base, TB), TB), :] = qraw[
                lax.div(tb, 2), rows, h * HD : (h + 1) * HD
            ]

    rows_of = 4 * RB * TB

    @pl.loop(0, lax.div(total + (RB - 1), RB))
    def _(rb):
        q = qs[rb]
        top = jnp.full((rows_of, 1), LOW, jnp.float32)
        acc = jnp.zeros((rows_of, 2 * HD), jnp.float32)

        def step(s, v, top, acc):
            new = jnp.maximum(top, jnp.max(s, axis=1, keepdims=True) * SCALE)
            p = jnp.exp2(s * SCALE - new).astype(jnp.bfloat16)
            acc = acc * jnp.exp2(top - new) + lax.dot_general(
                p, v, NN, preferred_element_type=jnp.float32
            )
            return new, acc

        if own:
            kv_rows = [okv[a, :, 0:512] for a in range(4)]
            keys = jnp.concatenate(
                [r[:, s * 256 : s * 256 + HD] for s in range(2) for r in kv_rows], axis=0
            )
            vals = jnp.concatenate(
                [r[:, s * 256 + HD : s * 256 + 2 * HD] for s in range(2) for r in kv_rows], axis=0
            )
            vals = jnp.concatenate([vals, jnp.ones((512, HD), jnp.bfloat16)], axis=1)
            s = lax.dot_general(q, keys, NT, preferred_element_type=jnp.float32)
            firsts, lasts = [], []
            for i in range(RB):
                slot, tb = place(rb * RB + i)
                first = jnp.full((TB, 1), slot * 256, jnp.int32)
                firsts.append(first)
                lasts.append(first + tb * TB + lax.broadcasted_iota(jnp.int32, (TB, 1), 0))
            first = jnp.concatenate(firsts * 4, axis=0)
            last = jnp.concatenate(lasts * 4, axis=0)
            place_of = lax.broadcasted_iota(jnp.int32, (rows_of, 512), 1)
            allowed = (place_of >= first) & (place_of <= last)
            s = jnp.where(allowed, s, LOW)
            new = jnp.max(s, axis=1, keepdims=True) * SCALE
            p = jnp.where(allowed, jnp.exp2(jnp.minimum(s * SCALE - new, 0.0)), 0.0)
            acc = lax.dot_general(
                p.astype(jnp.bfloat16), vals, NN, preferred_element_type=jnp.float32
            )
            top = new
        for half, kv in enumerate((kv0, kv1)):
            for j in range(2048 // KB):
                s = lax.dot_general(
                    q, kv[j * KB : (j + 1) * KB, 0:HD], NT, preferred_element_type=jnp.float32
                )
                start = half * 2048 + j * KB
                top, acc = step(s, v1[start : start + KB, :], top, acc)
        lane = lax.broadcasted_iota(jnp.int32, (TB, HD), 1)
        for i in range(RB):
            n = rb * RB + i

            @pl.when(n < total)
            def _(i=i, n=n):
                slot, tb = place(n)
                rows = pl.ds(pl.multiple_of(slot * 256 + tb * TB, TB), TB)
                st = jnp.zeros((TB, HD), jnp.float32)
                for h in range(4):
                    r = h * RB * TB + i * TB
                    a = acc[r : r + TB, :]
                    out[rows, h * HD : (h + 1) * HD] = a[:, 0:HD].astype(out.dtype)
                    t = jnp.broadcast_to(top[r : r + TB, :], (TB, HD))
                    for k, piece in enumerate(pieces(t) + pieces(a[:, HD : 2 * HD])):
                        st = jnp.where(lane == h * 8 + k, piece, st)
                if own:
                    stats[rows, :] = st.astype(jnp.bfloat16)
                else:
                    out[rows, 512:640] = st.astype(jnp.bfloat16)


def flash(shift, owner, lengths, info, bufs, kv0, kv1):
    own = shift == 0
    scratch = [pltpu.VMEM((4, 128, 512), jnp.bfloat16)]
    if own:
        scratch.append(pltpu.VMEM((4, 64, 512), jnp.bfloat16))
        out_shape = (
            jax.ShapeDtypeStruct((512, 512), jnp.float32),
            jax.ShapeDtypeStruct((512, 128), jnp.bfloat16),
        )
        out_specs = (VMEM, VMEM)
    else:
        out_shape = jax.ShapeDtypeStruct((512, 640), jnp.bfloat16)
        out_specs = VMEM
    scratch += [
        pltpu.VMEM((16 // RB, 4 * RB * TB, HD), jnp.bfloat16),
        pltpu.VMEM((4096, 2 * HD), jnp.bfloat16),
        pltpu.SemaphoreType.DMA((8,)),
    ]
    return pl.pallas_call(
        functools.partial(flash_kernel, shift, own),
        out_shape=out_shape,
        in_specs=[SMEM, SMEM, SMEM, ANY, ANY, ANY, ANY, VMEM, VMEM],
        out_specs=out_specs,
        scratch_shapes=scratch,
        compiler_params=pltpu.CompilerParams(vmem_limit_bytes=LIMIT),
        cost_estimate=pl.CostEstimate(
            flops=2 * 2 * 2048 * 4096 * 256, bytes_accessed=4 * 2**20, transcendentals=2048 * 4096
        ),
        name="flash_own" if own else "flash",
    )(owner, lengths, info, *bufs, kv0, kv1)


def combine_kernel(owner, lengths, info, acc, stats, g1, g2, g3, out):
    step = pl.program_id(0)
    len0, len1 = slot_lengths(owner, lengths, info[3])
    lane = lax.broadcasted_iota(jnp.int32, (HD, 1024), 0)
    col = lax.broadcasted_iota(jnp.int32, (HD, 1024), 1)
    kind = lane % 8 - 3 * (col // 512)
    pick = (lane // 8 == (col % 512) // HD) & (kind >= 0) & (kind < 3)
    pick = pick.astype(jnp.float32).astype(jnp.bfloat16)
    parts = [(acc[...], stats[...])] + [
        (g[:, 0:512].astype(jnp.float32), g[:, 512:640]) for g in (g1, g2, g3)
    ]
    wide = [lax.dot_general(st, pick, NN, preferred_element_type=jnp.float32) for _, st in parts]
    top = functools.reduce(jnp.maximum, [w[:, 0:512] for w in wide])
    numer, denom = 0.0, 0.0
    for (o, _), w in zip(parts, wide):
        f = jnp.exp2(w[:, 0:512] - top)
        numer = numer + o * f
        denom = denom + w[:, 512:1024] * f
    token = lax.rem(step, 2) * 128 + lax.broadcasted_iota(jnp.int32, (128, 1), 0)
    valid = token < jnp.where(step < 2, len0, len1)
    out[...] = jnp.where(valid, numer / denom, 0.0).astype(jnp.bfloat16)


def combine(owner, lengths, info, acc, stats, got):
    rows = lambda width: pl.BlockSpec((128, width), lambda i: (i, 0))
    return pl.pallas_call(
        combine_kernel,
        grid=(4,),
        out_shape=jax.ShapeDtypeStruct((512, 512), jnp.bfloat16),
        in_specs=[SMEM, SMEM, SMEM, rows(512), rows(128), rows(640), rows(640), rows(640)],
        out_specs=rows(512),
        compiler_params=pltpu.CompilerParams(vmem_limit_bytes=LIMIT),
        name="combine",
    )(owner, lengths, info, acc, stats, *got)


CORE = [(i, i ^ 1) for i in range(8)]


def along_x(shift):
    return [(i, (i + 2 * shift) % 8) for i in range(8)]


def local(queries, cand_kv, prefix_kv, lengths, owner):
    g = lax.axis_index("group")
    info = jnp.stack([lax.axis_index("prefix") // 2, g // 2, g % 2, g]).astype(jnp.int32)
    csend, kvsend = prep(info, queries, cand_kv, prefix_kv)
    crecv = lax.ppermute(csend, "group", CORE)
    b0, s1, s2, s3 = pack(owner, info, csend, crecv)
    b2 = lax.ppermute(s2, "group", along_x(2))
    b1 = lax.ppermute(s1, "group", along_x(1))
    b3 = lax.ppermute(s3, "group", along_x(3))
    bufs = (b0, b1, b2, b3)
    kv0 = lax.all_to_all(kvsend, "prefix", split_axis=0, concat_axis=0, tiled=True)
    kv0 = kv0.reshape(2048, 256)
    kv1 = lax.ppermute(kv0, "group", CORE)
    got = []
    for shift in (2, 1, 3):
        o = flash(shift, owner, lengths, info, bufs, kv0, kv1)
        got.append(lax.ppermute(o, "group", along_x(shift)))
    acc, stats = flash(0, owner, lengths, info, bufs, kv0, kv1)
    return combine(owner, lengths, info, acc, stats, got).reshape(2, 256, 512)


def solution(mesh):
    return jax.shard_map(
        local,
        mesh=mesh,
        in_specs=(P(None, "group", "prefix"), P(None, "group", None), P("prefix", None), P(), P()),
        out_specs=P("group", None, "prefix"),
        check_vma=False,
    )
```

```python
import functools
import math

import jax
import jax.numpy as jnp
from jax import lax
from jax.experimental import pallas as pl
from jax.experimental.pallas import tpu as pltpu
from jax.sharding import PartitionSpec as P

H = 64
KVH = 8
HD = 128
NT = (((1,), (1,)), ((), ()))
NN = (((1,), (0,)), ((), ()))
SCALE = math.log2(math.e) / math.sqrt(HD)
LOW = -1e30
VMEM = pl.BlockSpec(memory_space=pltpu.VMEM)
SMEM = pl.BlockSpec(memory_space=pltpu.SMEM)
ANY = pl.BlockSpec(memory_space=pl.ANY)
TB = 32
RB = 2
KB = 512


def prep_kernel(info, owner, cand, kv, kvsend, okvsend, slab, own, count, sem):
    head = pl.multiple_of(info[0] * HD, HD)
    rows = pl.ds(pl.multiple_of(info[3] * HD, HD), HD)
    copies = [
        pltpu.make_async_copy(kv.at[rows, :], slab, sem.at[0]),
        pltpu.make_async_copy(cand.at[:, :, pl.ds(head, HD)], own.at[:, :, 0:HD], sem.at[1]),
        pltpu.make_async_copy(
            cand.at[:, :, pl.ds(pl.multiple_of(head + KVH * HD, HD), HD)],
            own.at[:, :, HD : 2 * HD],
            sem.at[2],
        ),
    ]
    for copy in copies:
        copy.start()
    copies[0].wait()
    for dest in range(16):
        for half in range(2):
            column = (half * KVH + dest // 2) * HD
            kvsend[dest, :, half * HD : (half + 1) * HD] = slab[:, column : column + HD]
    copies[1].wait()
    copies[2].wait()
    for o in range(8):
        count[o] = 0
    for i in range(16):
        o = owner[i]
        slot = count[o]
        count[o] = slot + 1

        @pl.when(slot == 0)
        def _(i=i, o=o):
            okvsend[o, :, 0 : 2 * HD] = own[i]

        @pl.when(slot != 0)
        def _(i=i, o=o):
            okvsend[o, :, 2 * HD : 4 * HD] = own[i]


def prep(info, owner, cand, kv):
    return pl.pallas_call(
        prep_kernel,
        out_shape=(
            jax.ShapeDtypeStruct((16, 128, 256), jnp.bfloat16),
            jax.ShapeDtypeStruct((8, 32, 512), jnp.bfloat16),
        ),
        in_specs=[SMEM, SMEM, ANY, ANY],
        out_specs=(VMEM, VMEM),
        scratch_shapes=[
            pltpu.VMEM((HD, 2048), jnp.bfloat16),
            pltpu.VMEM((16, 32, 256), jnp.bfloat16),
            pltpu.SMEM((8,), jnp.int32),
            pltpu.SemaphoreType.DMA((3,)),
        ],
        compiler_params=pltpu.CompilerParams(vmem_limit_bytes=8 * 2**20),
        name="prep",
    )(info, owner, cand, kv)


def slots(owner, lengths, group):
    first, second, seen = 0, 0, 0
    len0, len1 = 0, 0
    for i in range(16):
        hit = owner[i] == group
        is0, is1 = hit & (seen == 0), hit & (seen == 1)
        first, len0 = jnp.where(is0, i, first), jnp.where(is0, lengths[i], len0)
        second, len1 = jnp.where(is1, i, second), jnp.where(is1, lengths[i], len1)
        seen = seen + hit.astype(jnp.int32)
    return (first, len0), (second, len1)


def packed_stats(tops, totals):
    lane = lax.rem(lax.broadcasted_iota(jnp.int32, (TB, HD), 1), 32)
    head, kind = lax.div(lane, 8), lax.rem(lane, 8)
    value = jnp.zeros((TB, HD), jnp.float32)
    for h in range(4):
        value = jnp.where(head == h, jnp.where(kind < 3, tops[h], totals[h]), value)
    hi = value.astype(jnp.bfloat16).astype(jnp.float32)
    mid = (value - hi).astype(jnp.bfloat16).astype(jnp.float32)
    piece = lax.rem(kind, 3)
    value = jnp.where(piece == 0, hi, jnp.where(piece == 1, mid, value - hi - mid))
    return jnp.where(kind < 6, value, 0.0)


def flash_kernel(shifts, own, owner, lengths, info, *rest):
    bufs, rest = rest[:8], rest[8:]
    kv0, kv1 = rest[:2]
    rest = rest[2:]
    if own:
        okv, out, stats = rest[:3]
        rest = rest[3:]
    else:
        outs, rest = rest[: len(shifts)], rest[len(shifts) :]
        hold, rest = rest[0], rest[1:]
    qraw, qs, v1, sem = rest
    x, core = info[1], info[2]
    passages = []
    for shift in shifts:
        passages += slots(owner, lengths, lax.rem(x + shift, 4) * 2 + core)
    copies = []
    for b in range(8):
        tb = lax.rem(x + 4 - b // 2, 4) * 2 + lax.rem(core + b, 2)
        for k, (i, _) in enumerate(passages):
            copies.append(
                pltpu.make_async_copy(bufs[b].at[i], qraw.at[k * 8 + tb], sem.at[b * 4 + k])
            )
    for c in copies:
        c.start()
    for half, kv in enumerate((kv0, kv1)):
        v1[half * 2048 : (half + 1) * 2048, 0:HD] = kv[:, HD : 2 * HD]
    v1[:, HD : 2 * HD] = jnp.ones((4096, HD), jnp.bfloat16)
    firsts, total = [], 0
    for _, length in passages:
        firsts.append(total)
        total = total + lax.div(length + (TB - 1), TB)
    for c in copies:
        c.wait()

    def place(n):
        k, first = 0, 0
        for j in range(1, len(firsts)):
            k = jnp.where(n >= firsts[j], j, k)
            first = jnp.where(n >= firsts[j], firsts[j], first)
        return k, n - first

    @pl.loop(0, total)
    def _(n):
        k, tb = place(n)
        base = lax.rem(n, RB) * TB
        for h in range(4):
            qs[lax.div(n, RB), pl.ds(pl.multiple_of(h * RB * TB + base, TB), TB), :] = qraw[
                k * 8 + tb, :, h * HD : (h + 1) * HD
            ]

    rows_of = 4 * RB * TB

    @pl.loop(0, lax.div(total + (RB - 1), RB))
    def _(rb):
        q = qs[rb]
        if own:
            keys = jnp.concatenate(
                [okv[t, :, s * 256 : s * 256 + HD] for s in range(2) for t in range(8)], axis=0
            )
            vals = jnp.concatenate(
                [okv[t, :, s * 256 + HD : s * 256 + 2 * HD] for s in range(2) for t in range(8)],
                axis=0,
            )
            vals = jnp.concatenate([vals, jnp.ones((512, HD), jnp.bfloat16)], axis=1)
            s = lax.dot_general(q, keys, NT, preferred_element_type=jnp.float32)
            starts, ends = [], []
            for i in range(RB):
                k, tb = place(rb * RB + i)
                start = jnp.full((TB, 1), k * 256, jnp.int32)
                starts.append(start)
                ends.append(start + tb * TB + lax.broadcasted_iota(jnp.int32, (TB, 1), 0))
            start = jnp.concatenate(starts * 4, axis=0)
            end = jnp.concatenate(ends * 4, axis=0)
            key_of = lax.broadcasted_iota(jnp.int32, (rows_of, 512), 1)
            allowed = (key_of >= start) & (key_of <= end)
            s = jnp.where(allowed, s, LOW)
            top = jnp.max(s, axis=1, keepdims=True) * SCALE
            p = jnp.where(allowed, jnp.exp2(jnp.minimum(s * SCALE - top, 0.0)), 0.0)
            acc = lax.dot_general(
                p.astype(jnp.bfloat16), vals, NN, preferred_element_type=jnp.float32
            )
            top = jnp.broadcast_to(top, (rows_of, HD))
        else:
            top = jnp.full((rows_of, HD), LOW, jnp.float32)
            acc = jnp.zeros((rows_of, 2 * HD), jnp.float32)
        for half, kv in enumerate((kv0, kv1)):
            for j in range(2048 // KB):
                keys = kv[j * KB : (j + 1) * KB, 0:HD]
                s = lax.dot_general(q, keys, NT, preferred_element_type=jnp.float32)
                new = jnp.maximum(top, jnp.max(s, axis=1, keepdims=True) * SCALE)
                p = jnp.exp2(s * SCALE - new[:, 0:1]).astype(jnp.bfloat16)
                fade = jnp.exp2(top - new)
                start = half * 2048 + j * KB
                acc = acc * jnp.concatenate([fade, fade], axis=1) + lax.dot_general(
                    p, v1[start : start + KB, :], NN, preferred_element_type=jnp.float32
                )
                top = new
        for i in range(RB):
            n = rb * RB + i

            @pl.when(n < total)
            def _(i=i, n=n):
                k, tb = place(n)
                block = lax.rem(k, 2) * 8 + tb
                rows = pl.ds(pl.multiple_of(block * TB, TB), TB)
                tops, totals = [], []
                for h in range(4):
                    r = h * RB * TB + i * TB
                    value = acc[r : r + TB, 0:HD]
                    if own:
                        out[rows, h * HD : (h + 1) * HD] = value
                    else:
                        hold[lax.div(k, 2), rows, h * HD : (h + 1) * HD] = value.astype(
                            jnp.bfloat16
                        )
                    tops.append(top[r : r + TB, :])
                    totals.append(acc[r : r + TB, HD : 2 * HD])
                st = packed_stats(tops, totals)
                lane = lax.broadcasted_iota(jnp.int32, (TB, HD), 1)
                mine = lax.div(lane, 32) == lax.rem(block, 4)
                for group in range(4):

                    @pl.when(lax.div(block, 4) == group)
                    def _(group=group):
                        columns = slice(group * HD, (group + 1) * HD)
                        if own:
                            old = stats[:, columns].astype(jnp.float32)
                            stats[:, columns] = jnp.where(mine, st, old).astype(jnp.bfloat16)
                        else:
                            d = lax.div(k, 2)
                            old = hold[d, 512:544, columns].astype(jnp.float32)
                            hold[d, 512:544, columns] = jnp.where(mine, st, old).astype(
                                jnp.bfloat16
                            )

    if not own:
        copies = [
            pltpu.make_async_copy(hold.at[d], outs[d], sem.at[d]) for d in range(len(shifts))
        ]
        for c in copies:
            c.start()
        for c in copies:
            c.wait()


def flash(shifts, owner, lengths, info, bufs, kv0, kv1, okv=None):
    own = okv is not None
    dests = len(shifts)
    scratch = []
    if own:
        out_shape = (
            jax.ShapeDtypeStruct((512, 512), jnp.float32),
            jax.ShapeDtypeStruct((32, 512), jnp.bfloat16),
        )
        out_specs = (VMEM, VMEM)
    else:
        out_shape = (jax.ShapeDtypeStruct((544, 512), jnp.bfloat16),) * dests
        out_specs = (ANY,) * dests
        scratch.append(pltpu.VMEM((dests, 544, 512), jnp.bfloat16))
    scratch += [
        pltpu.VMEM((16 * dests, 32, 512), jnp.bfloat16),
        pltpu.VMEM((16 * dests // RB, 4 * RB * TB, HD), jnp.bfloat16),
        pltpu.VMEM((4096, 2 * HD), jnp.bfloat16),
        pltpu.SemaphoreType.DMA((32,)),
    ]
    return pl.pallas_call(
        functools.partial(flash_kernel, shifts, own),
        out_shape=out_shape,
        in_specs=[SMEM, SMEM, SMEM] + [ANY] * 8 + [VMEM] * (3 if own else 2),
        out_specs=out_specs,
        scratch_shapes=scratch,
        compiler_params=pltpu.CompilerParams(vmem_limit_bytes=28 * 2**20),
        cost_estimate=pl.CostEstimate(
            flops=dests * 2 * 2 * 2048 * 4096 * 256,
            bytes_accessed=4 * 2**20,
            transcendentals=dests * 2048 * 4096,
        ),
        name="flash_own" if own else f"flash_{dests}",
    )(owner, lengths, info, *bufs, kv0, kv1, *([okv] if own else []))


def combine_kernel(owner, lengths, info, acc, stats, g1, s1, g2, s2, g3, s3, out):
    step = pl.program_id(0)
    (_, len0), (_, len1) = slots(owner, lengths, info[3])
    lane = lax.rem(lax.broadcasted_iota(jnp.int32, (HD, 1024), 0), 32)
    col = lax.broadcasted_iota(jnp.int32, (HD, 1024), 1)
    kind = lax.rem(lane, 8) - 3 * lax.div(col, 512)
    pick = (lax.div(lane, 8) == lax.div(lax.rem(col, 512), HD)) & (kind >= 0) & (kind < 3)
    pick = pick.astype(jnp.float32).astype(jnp.bfloat16)
    group = lax.div(lax.broadcasted_iota(jnp.int32, (TB, HD), 1), 32)
    token = lax.rem(step, 2) * 128 + lax.broadcasted_iota(jnp.int32, (128, 1), 0)
    valid = token < jnp.where(step < 2, len0, len1)
    wide = []
    for st in (stats, s1, s2, s3):
        st = st[...].astype(jnp.float32)
        st = jnp.concatenate([jnp.where(group == i, st, 0.0) for i in range(4)], axis=0)
        wide.append(
            lax.dot_general(
                st.astype(jnp.bfloat16), pick, NN, preferred_element_type=jnp.float32
            )
        )
    top = functools.reduce(jnp.maximum, [w[:, 0:512] for w in wide])
    numer, denom = 0.0, 0.0
    for o, w in zip((acc, g1, g2, g3), wide):
        f = jnp.exp2(w[:, 0:512] - top)
        numer = numer + o[...].astype(jnp.float32) * f
        denom = denom + w[:, 512:1024] * f
    out[...] = jnp.where(valid, numer / denom, 0.0).astype(jnp.bfloat16)


def combine(owner, lengths, info, acc, stats, got):
    part = pl.BlockSpec((128, 512), lambda i: (i, 0))
    tail = pl.BlockSpec((32, 128), lambda i: (16, i))
    return pl.pallas_call(
        combine_kernel,
        grid=(4,),
        out_shape=jax.ShapeDtypeStruct((512, 512), jnp.bfloat16),
        in_specs=[SMEM, SMEM, SMEM, part, pl.BlockSpec((32, 128), lambda i: (0, i))]
        + [part, tail] * 3,
        out_specs=part,
        compiler_params=pltpu.CompilerParams(vmem_limit_bytes=16 * 2**20),
        name="combine",
    )(owner, lengths, info, acc, stats, *(a for g in got for a in (g, g)))


CORE = [(i, i ^ 1) for i in range(8)]


def along_x(shift):
    return [(i, (i + 2 * shift) % 8) for i in range(8)]


def local(queries, cand_kv, prefix_kv, lengths, owner):
    g = lax.axis_index("group")
    info = jnp.stack([lax.axis_index("prefix") // 2, g // 2, g % 2, g]).astype(jnp.int32)
    from_x = [lax.ppermute(queries, "group", along_x(shift)) for shift in (1, 2, 3)]
    kvsend, okvsend = prep(info, owner, cand_kv, prefix_kv)
    kv0 = lax.all_to_all(kvsend, "prefix", split_axis=0, concat_axis=0, tiled=True)
    kv0 = kv0.reshape(2048, 256)
    kv1 = lax.ppermute(kv0, "group", CORE)
    bufs = []
    for a in [queries] + from_x:
        bufs += [a, lax.ppermute(a, "group", CORE)]
    (o2,) = flash((2,), owner, lengths, info, bufs, kv0, kv1)
    got2 = lax.ppermute(o2, "group", along_x(2))
    o1, o3 = flash((1, 3), owner, lengths, info, bufs, kv0, kv1)
    got1 = lax.ppermute(o1, "group", along_x(1))
    got3 = lax.ppermute(o3, "group", along_x(3))
    okvsend, _ = lax.optimization_barrier((okvsend, kv0))
    okv = lax.all_to_all(okvsend, "group", split_axis=0, concat_axis=0, tiled=True)
    acc, stats = flash((0,), owner, lengths, info, bufs, kv0, kv1, okv)
    return combine(owner, lengths, info, acc, stats, (got1, got2, got3)).reshape(2, 256, 512)


def solution(mesh):
    return jax.shard_map(
        local,
        mesh=mesh,
        in_specs=(P(None, "group", "prefix"), P(None, "group", None), P("prefix", None), P(), P()),
        out_specs=P("group", None, "prefix"),
        check_vma=False,
    )
```

```python
import functools
import math

import jax
import jax.numpy as jnp
from jax import lax
from jax.experimental import pallas as pl
from jax.experimental.pallas import tpu as pltpu
from jax.sharding import PartitionSpec as P

H = 64
KVH = 8
HD = 128
NT = (((1,), (1,)), ((), ()))
NN = (((1,), (0,)), ((), ()))
SCALE = math.log2(math.e) / math.sqrt(HD)
LOW = -1e30
LIMIT = 60 * 2**20
VMEM = pl.BlockSpec(memory_space=pltpu.VMEM)
SMEM = pl.BlockSpec(memory_space=pltpu.SMEM)
ANY = pl.BlockSpec(memory_space=pl.ANY)
TB = 32
RB = 4
KB = 256


def prep_kernel(info, owner, cand, kv, kvsend, okvsend, slab, own, count, sem):
    head = pl.multiple_of(info[0] * HD, HD)
    rows = pl.ds(pl.multiple_of(info[3] * HD, HD), HD)
    copies = [
        pltpu.make_async_copy(kv.at[rows, :], slab, sem.at[0]),
        pltpu.make_async_copy(cand.at[:, :, pl.ds(head, HD)], own.at[:, :, 0:HD], sem.at[1]),
        pltpu.make_async_copy(
            cand.at[:, :, pl.ds(pl.multiple_of(head + KVH * HD, HD), HD)],
            own.at[:, :, HD : 2 * HD],
            sem.at[2],
        ),
    ]
    for copy in copies:
        copy.start()
    copies[0].wait()
    for dest in range(16):
        for half in range(2):
            column = (half * KVH + dest // 2) * HD
            kvsend[dest, :, half * HD : (half + 1) * HD] = slab[:, column : column + HD]
    copies[1].wait()
    copies[2].wait()
    for o in range(8):
        count[o] = 0
    for i in range(16):
        o = owner[i]
        slot = count[o]
        count[o] = slot + 1

        @pl.when(slot == 0)
        def _(i=i, o=o):
            okvsend[o, :, 0 : 2 * HD] = own[i]

        @pl.when(slot != 0)
        def _(i=i, o=o):
            okvsend[o, :, 2 * HD : 4 * HD] = own[i]


def prep(info, owner, cand, kv):
    return pl.pallas_call(
        prep_kernel,
        out_shape=(
            jax.ShapeDtypeStruct((16, 128, 256), jnp.bfloat16),
            jax.ShapeDtypeStruct((8, 32, 512), jnp.bfloat16),
        ),
        in_specs=[SMEM, SMEM, ANY, ANY],
        out_specs=(VMEM, VMEM),
        scratch_shapes=[
            pltpu.VMEM((HD, 2048), jnp.bfloat16),
            pltpu.VMEM((16, 32, 256), jnp.bfloat16),
            pltpu.SMEM((8,), jnp.int32),
            pltpu.SemaphoreType.DMA((3,)),
        ],
        compiler_params=pltpu.CompilerParams(vmem_limit_bytes=LIMIT),
        name="prep",
    )(info, owner, cand, kv)


def slots(owner, lengths, group):
    first, second, seen = 0, 0, 0
    len0, len1 = 0, 0
    for i in range(16):
        hit = owner[i] == group
        is0, is1 = hit & (seen == 0), hit & (seen == 1)
        first, len0 = jnp.where(is0, i, first), jnp.where(is0, lengths[i], len0)
        second, len1 = jnp.where(is1, i, second), jnp.where(is1, lengths[i], len1)
        seen = seen + hit.astype(jnp.int32)
    return (first, len0), (second, len1)


def packed_stats(tops, totals):
    lane = lax.rem(lax.broadcasted_iota(jnp.int32, (TB, HD), 1), 32)
    head, kind = lax.div(lane, 8), lax.rem(lane, 8)
    value = jnp.zeros((TB, HD), jnp.float32)
    for h in range(4):
        value = jnp.where(head == h, jnp.where(kind < 3, tops[h], totals[h]), value)
    hi = value.astype(jnp.bfloat16).astype(jnp.float32)
    mid = (value - hi).astype(jnp.bfloat16).astype(jnp.float32)
    piece = lax.rem(kind, 3)
    value = jnp.where(piece == 0, hi, jnp.where(piece == 1, mid, value - hi - mid))
    return jnp.where(kind < 6, value, 0.0)


def flash_kernel(shifts, own, owner, lengths, info, *rest):
    bufs, rest = rest[:10], rest[10:]
    kv0, kv1 = rest[:2]
    rest = rest[2:]
    if own:
        okv, out, stats = rest[:3]
        rest = rest[3:]
        okeys, ovals, rest = rest[0], rest[1], rest[2:]
    else:
        outs, rest = rest[: len(shifts)], rest[len(shifts) :]
    hold, held, qraw, qs, k1, v1, sem = rest
    x, core = info[1], info[2]
    passages = []
    for shift in shifts:
        passages += slots(owner, lengths, lax.rem(x + shift, 4) * 2 + core)
    copies = []
    for b in range(8):
        tb = lax.rem(x + (0, 3, 1, 2)[b // 2], 4) * 2 + lax.rem(core + b, 2)
        for k, (i, _) in enumerate(passages):
            into, done = qraw.at[k * 8 + tb], sem.at[b * 4 + k]
            if b < 6:
                copies.append(pltpu.make_async_copy(bufs[b].at[i], into, done))
                copies[-1].start()
            else:
                lower = pltpu.make_async_copy(bufs[b].at[lax.rem(i, 8)], into, done)
                upper = pltpu.make_async_copy(bufs[b + 2].at[lax.rem(i, 8)], into, done)
                pl.when(i < 8)(lower.start)
                pl.when(i >= 8)(upper.start)
                copies.append(lower)
    loads = []
    for half, kv in enumerate((kv0, kv1)):
        rows = pl.ds(half * 2048, 2048)
        for part, (column, into) in enumerate(((0, k1.at[rows, 0:HD]), (0, k1.at[rows, HD : 2 * HD]), (HD, v1.at[rows, 0:HD]))):
            loads.append(
                pltpu.make_async_copy(kv.at[:, column : column + HD], into, sem.at[32 + half * 3 + part])
            )
            loads[-1].start()
    v1[:, HD : 2 * HD] = jnp.ones((4096, HD), jnp.bfloat16)
    if own:
        for s in range(2):
            for t in range(8):
                rows = slice(s * 256 + t * TB, s * 256 + (t + 1) * TB)
                key = okv[t, :, s * 256 : s * 256 + HD]
                okeys[rows, 0:HD] = key
                okeys[rows, HD : 2 * HD] = key
                ovals[rows, 0:HD] = okv[t, :, s * 256 + HD : s * 256 + 2 * HD]
        ovals[:, HD : 2 * HD] = jnp.ones((512, HD), jnp.bfloat16)
    firsts, total = [], 0
    for _, length in passages:
        firsts.append(total)
        total = total + lax.div(length + (TB - 1), TB)
    for c in copies:
        c.wait()

    def place(n):
        k, first = 0, 0
        for j in range(1, len(firsts)):
            k = jnp.where(n >= firsts[j], j, k)
            first = jnp.where(n >= firsts[j], firsts[j], first)
        return k, n - first

    @pl.loop(0, total)
    def _(n):
        k, tb = place(n)
        base = lax.rem(n, RB) * TB
        for h in range(4):
            rows = pl.ds(pl.multiple_of(h * RB * TB + base, TB), TB)
            scaled = qraw[k * 8 + tb, :, h * HD : (h + 1) * HD].astype(jnp.float32) * SCALE
            high = scaled.astype(jnp.bfloat16)
            qs[lax.div(n, RB), rows, 0:HD] = high
            qs[lax.div(n, RB), rows, HD : 2 * HD] = (scaled - high.astype(jnp.float32)).astype(
                jnp.bfloat16
            )

    for c in loads:
        c.wait()

    rows_of = 4 * RB * TB

    @pl.loop(0, lax.div(total + (RB - 1), RB))
    def _(rb):
        q = qs[rb]
        if own:
            s = lax.dot_general(q, okeys[...], NT, preferred_element_type=jnp.float32)
            starts, ends = [], []
            for i in range(RB):
                k, tb = place(rb * RB + i)
                start = jnp.full((TB, 1), k * 256, jnp.int32)
                starts.append(start)
                ends.append(start + tb * TB + lax.broadcasted_iota(jnp.int32, (TB, 1), 0))
            start = jnp.concatenate(starts * 4, axis=0)
            end = jnp.concatenate(ends * 4, axis=0)
            key_of = lax.broadcasted_iota(jnp.int32, (rows_of, 512), 1)
            allowed = (key_of >= start) & (key_of <= end)
            s = jnp.where(allowed, s, LOW)
            top = jnp.max(s, axis=1, keepdims=True)
            p = jnp.where(allowed, jnp.exp2(jnp.minimum(s - top, 0.0)), 0.0)
            acc = lax.dot_general(
                p.astype(jnp.bfloat16), ovals[...], NN, preferred_element_type=jnp.float32
            )
            top = jnp.broadcast_to(top, (rows_of, HD))
        else:
            top = jnp.full((rows_of, HD), LOW, jnp.float32)
            acc = jnp.zeros((rows_of, 2 * HD), jnp.float32)
        for j in range(4096 // KB):
            rows = slice(j * KB, (j + 1) * KB)
            s = lax.dot_general(q, k1[rows, :], NT, preferred_element_type=jnp.float32)
            new = jnp.maximum(top, jnp.max(s, axis=1, keepdims=True))
            p = jnp.exp2(s - new[:, 0:1]).astype(jnp.bfloat16)
            fade = jnp.exp2(top - new)
            acc = acc * jnp.concatenate([fade, fade], axis=1) + lax.dot_general(
                p, v1[rows, :], NN, preferred_element_type=jnp.float32
            )
            top = new
        for i in range(RB):
            n = rb * RB + i
            k, tb = place(n)
            block = jnp.where(n < total, lax.rem(k, 2) * 8 + tb, 16)
            d = lax.div(k, 2)
            rows = pl.ds(pl.multiple_of(block * TB, TB), TB)
            tops, totals = [], []
            for h in range(4):
                r = h * RB * TB + i * TB
                hold[d, rows, h * HD : (h + 1) * HD] = acc[r : r + TB, 0:HD].astype(hold.dtype)
                tops.append(top[r : r + TB, :])
                totals.append(acc[r : r + TB, HD : 2 * HD])
            lane = lax.broadcasted_iota(jnp.int32, (TB, HD), 1)
            group = lax.div(block, 4)
            held[d, group] = jnp.where(
                lax.div(lane, 32) == lax.rem(block, 4), packed_stats(tops, totals), held[d, group]
            )

    copies = []
    for d in range(len(shifts)):
        if own:
            for group in range(4):
                stats[:, group * HD : (group + 1) * HD] = held[d, group].astype(jnp.bfloat16)
            copies.append(pltpu.make_async_copy(hold.at[d, 0:512, :], out, sem.at[d]))
        else:
            for group in range(4):
                hold[d, 512:544, group * HD : (group + 1) * HD] = held[d, group].astype(
                    jnp.bfloat16
                )
            copies.append(pltpu.make_async_copy(hold.at[d], outs[d], sem.at[d]))
        copies[-1].start()
    for c in copies:
        c.wait()


def flash(shifts, owner, lengths, info, bufs, kv0, kv1, okv=None):
    own = okv is not None
    dests = len(shifts)
    scratch = []
    if own:
        out_shape = (
            jax.ShapeDtypeStruct((512, 512), jnp.float32),
            jax.ShapeDtypeStruct((32, 512), jnp.bfloat16),
        )
        out_specs = (ANY, VMEM)
        scratch += [pltpu.VMEM((512, 2 * HD), jnp.bfloat16)] * 2
    else:
        out_shape = (jax.ShapeDtypeStruct((544, 512), jnp.bfloat16),) * dests
        out_specs = (ANY,) * dests
    scratch += [
        pltpu.VMEM((dests, 544, 512), jnp.float32 if own else jnp.bfloat16),
        pltpu.VMEM((dests, 5, TB, HD), jnp.float32),
        pltpu.VMEM((16 * dests, 32, 512), jnp.bfloat16),
        pltpu.VMEM((16 * dests // RB, 4 * RB * TB, 2 * HD), jnp.bfloat16),
        pltpu.VMEM((4096, 2 * HD), jnp.bfloat16),
        pltpu.VMEM((4096, 2 * HD), jnp.bfloat16),
        pltpu.SemaphoreType.DMA((38,)),
    ]
    return pl.pallas_call(
        functools.partial(flash_kernel, shifts, own),
        out_shape=out_shape,
        in_specs=[SMEM, SMEM, SMEM] + [ANY] * 12 + [VMEM] * own,
        out_specs=out_specs,
        scratch_shapes=scratch,
        compiler_params=pltpu.CompilerParams(vmem_limit_bytes=LIMIT),
        cost_estimate=pl.CostEstimate(
            flops=dests * 2 * 2 * 2048 * 4096 * 256,
            bytes_accessed=4 * 2**20,
            transcendentals=dests * 2048 * 4096,
        ),
        name="flash_own" if own else f"flash_{dests}",
    )(owner, lengths, info, *bufs, kv0, kv1, *([okv] if own else []))


def combine_kernel(owner, lengths, info, acc, stats, g1, s1, g2, s2, g3, s3, out):
    step = pl.program_id(0)
    (_, len0), (_, len1) = slots(owner, lengths, info[3])
    lane = lax.rem(lax.broadcasted_iota(jnp.int32, (HD, 1024), 0), 32)
    col = lax.broadcasted_iota(jnp.int32, (HD, 1024), 1)
    kind = lax.rem(lane, 8) - 3 * lax.div(col, 512)
    pick = (lax.div(lane, 8) == lax.div(lax.rem(col, 512), HD)) & (kind >= 0) & (kind < 3)
    pick = pick.astype(jnp.float32).astype(jnp.bfloat16)
    group = lax.div(lax.broadcasted_iota(jnp.int32, (TB, HD), 1), 32)
    token = lax.rem(step, 2) * 128 + lax.broadcasted_iota(jnp.int32, (128, 1), 0)
    valid = token < jnp.where(step < 2, len0, len1)
    wide = []
    for st in (stats, s1, s2, s3):
        st = st[...].astype(jnp.float32)
        st = jnp.concatenate([jnp.where(group == i, st, 0.0) for i in range(4)], axis=0)
        wide.append(
            lax.dot_general(
                st.astype(jnp.bfloat16), pick, NN, preferred_element_type=jnp.float32
            )
        )
    top = functools.reduce(jnp.maximum, [w[:, 0:512] for w in wide])
    numer, denom = 0.0, 0.0
    for o, w in zip((acc, g1, g2, g3), wide):
        f = jnp.exp2(w[:, 0:512] - top)
        numer = numer + o[...].astype(jnp.float32) * f
        denom = denom + w[:, 512:1024] * f
    out[...] = jnp.where(valid, numer / denom, 0.0).astype(jnp.bfloat16)


def combine(owner, lengths, info, acc, stats, got):
    part = pl.BlockSpec((128, 512), lambda i: (i, 0))
    tail = pl.BlockSpec((32, 128), lambda i: (16, i))
    return pl.pallas_call(
        combine_kernel,
        grid=(4,),
        out_shape=jax.ShapeDtypeStruct((512, 512), jnp.bfloat16),
        in_specs=[SMEM, SMEM, SMEM, part, pl.BlockSpec((32, 128), lambda i: (0, i))]
        + [part, tail] * 3,
        out_specs=part,
        compiler_params=pltpu.CompilerParams(vmem_limit_bytes=LIMIT),
        name="combine",
    )(owner, lengths, info, acc, stats, *(a for g in got for a in (g, g)))


def split_kernel(left, right, lower, upper, sem):
    copies = [
        pltpu.make_async_copy(left.at[0:8], lower, sem.at[0]),
        pltpu.make_async_copy(right.at[8:16], upper, sem.at[1]),
    ]
    for c in copies:
        c.start()
    for c in copies:
        c.wait()


def split(left, right):
    return pl.pallas_call(
        split_kernel,
        out_shape=(jax.ShapeDtypeStruct((8, 32, 512), jnp.bfloat16),) * 2,
        in_specs=[ANY, ANY],
        out_specs=(VMEM, VMEM),
        scratch_shapes=[pltpu.SemaphoreType.DMA((2,))],
        compiler_params=pltpu.CompilerParams(vmem_limit_bytes=4 * 2**20),
        cost_estimate=pl.CostEstimate(
            flops=2 * 10**11, bytes_accessed=2**20, transcendentals=0
        ),
        name="split",
    )(left, right)


CORE = [(i, i ^ 1) for i in range(8)]


def along_x(shift):
    return [(i, (i + 2 * shift) % 8) for i in range(8)]


def local(queries, cand_kv, prefix_kv, lengths, owner):
    g = lax.axis_index("group")
    info = jnp.stack([lax.axis_index("prefix") // 2, g // 2, g % 2, g]).astype(jnp.int32)
    swap = lambda a: lax.ppermute(a, "group", CORE)
    pairs = lambda a: [a, swap(a)]
    left = lax.ppermute(queries, "group", along_x(1))
    right = lax.ppermute(queries, "group", along_x(3))
    kvsend, okvsend = prep(info, owner, cand_kv, prefix_kv)
    kv0 = lax.all_to_all(kvsend, "prefix", split_axis=0, concat_axis=0, tiled=True)
    lower, upper = split(left, right)
    lower = lax.ppermute(lower, "group", along_x(1))
    upper = lax.ppermute(upper, "group", along_x(3))
    kv0, lower, upper = lax.optimization_barrier((kv0, lower, upper))
    kv0 = kv0.reshape(2048, 256)
    kv1 = swap(kv0)
    bufs = pairs(queries) + pairs(left) + pairs(right) + pairs(lower) + pairs(upper)
    (o2,) = flash((2,), owner, lengths, info, bufs, kv0, kv1)
    got2 = lax.ppermute(o2, "group", along_x(2))
    o1, o3 = flash((1, 3), owner, lengths, info, bufs, kv0, kv1)
    got1 = lax.ppermute(o1, "group", along_x(1))
    got3 = lax.ppermute(o3, "group", along_x(3))
    okvsend, _ = lax.optimization_barrier((okvsend, kv0))
    okv = lax.all_to_all(okvsend, "group", split_axis=0, concat_axis=0, tiled=True)
    acc, stats = flash((0,), owner, lengths, info, bufs, kv0, kv1, okv)
    return combine(owner, lengths, info, acc, stats, (got1, got2, got3)).reshape(2, 256, 512)


def solution(mesh):
    return jax.shard_map(
        local,
        mesh=mesh,
        in_specs=(P(None, "group", "prefix"), P(None, "group", None), P("prefix", None), P(), P()),
        out_specs=P("group", None, "prefix"),
        check_vma=False,
    )
```

```python
import functools
import math

import jax
import jax.numpy as jnp
from jax import lax
from jax.experimental import pallas as pl
from jax.experimental.pallas import tpu as pltpu
from jax.sharding import PartitionSpec as P

H = 64
KVH = 8
HD = 128
NT = (((1,), (1,)), ((), ()))
NN = (((1,), (0,)), ((), ()))
SCALE = math.log2(math.e) / math.sqrt(HD)
LOW = -1e30
LIMIT = 60 * 2**20
VMEM = pl.BlockSpec(memory_space=pltpu.VMEM)
SMEM = pl.BlockSpec(memory_space=pltpu.SMEM)
ANY = pl.BlockSpec(memory_space=pl.ANY)
TB = 32
RB = 8
KB = 256


def prep_kernel(info, owner, cand, kv, kvsend, okvsend, slab, own, count, sem):
    head = pl.multiple_of(info[0] * HD, HD)
    rows = pl.ds(pl.multiple_of(info[3] * HD, HD), HD)
    copies = [
        pltpu.make_async_copy(kv.at[rows, :], slab, sem.at[0]),
        pltpu.make_async_copy(cand.at[:, :, pl.ds(head, HD)], own.at[:, :, 0:HD], sem.at[1]),
        pltpu.make_async_copy(
            cand.at[:, :, pl.ds(pl.multiple_of(head + KVH * HD, HD), HD)],
            own.at[:, :, HD : 2 * HD],
            sem.at[2],
        ),
    ]
    for copy in copies:
        copy.start()
    copies[0].wait()
    for dest in range(16):
        for half in range(2):
            column = (half * KVH + dest // 2) * HD
            kvsend[dest, :, half * HD : (half + 1) * HD] = slab[:, column : column + HD]
    copies[1].wait()
    copies[2].wait()
    for o in range(8):
        count[o] = 0
    for i in range(16):
        o = owner[i]
        slot = lax.rem(o, 2) * 2 + count[o]
        count[o] = count[o] + 1
        for s in range(4):

            @pl.when(slot == s)
            def _(i=i, s=s, x=lax.div(o, 2)):
                for core in range(2):
                    okvsend[x * 2 + core, :, s * 256 : (s + 1) * 256] = own[i]


def prep(info, owner, cand, kv):
    return pl.pallas_call(
        prep_kernel,
        out_shape=(
            jax.ShapeDtypeStruct((16, 128, 256), jnp.bfloat16),
            jax.ShapeDtypeStruct((8, 32, 1024), jnp.bfloat16),
        ),
        in_specs=[SMEM, SMEM, ANY, ANY],
        out_specs=(VMEM, VMEM),
        scratch_shapes=[
            pltpu.VMEM((HD, 2048), jnp.bfloat16),
            pltpu.VMEM((16, 32, 256), jnp.bfloat16),
            pltpu.SMEM((8,), jnp.int32),
            pltpu.SemaphoreType.DMA((3,)),
        ],
        compiler_params=pltpu.CompilerParams(vmem_limit_bytes=LIMIT),
        name="prep",
    )(info, owner, cand, kv)


def rank(owner, place, count):
    for o in range(8):
        count[o] = 0
    for i in range(16):
        o = owner[i]
        place[o * 2 + count[o]] = i
        count[o] = count[o] + 1


def blocks_of(length, core):
    return lax.div(length - TB * core + (2 * TB - 1), 2 * TB)


def packed_stats(tops, totals):
    lane = lax.rem(lax.broadcasted_iota(jnp.int32, (TB, HD), 1), 16)
    head, kind = lax.div(lane, 8), lax.rem(lane, 8)
    first, second = (jnp.where(kind < 3, tops[h], totals[h]) for h in range(2))
    value = jnp.where(head == 0, first, second)
    hi = value.astype(jnp.bfloat16).astype(jnp.float32)
    mid = (value - hi).astype(jnp.bfloat16).astype(jnp.float32)
    piece = lax.rem(kind, 3)
    value = jnp.where(piece == 0, hi, jnp.where(piece == 1, mid, value - hi - mid))
    return jnp.where(kind < 6, value, 0.0)


def load_queries(bufs, x, columns, qraw, sem):
    into = [qraw.at[lax.rem(x + shift, 4)] for shift in (0, 3, 1)]
    into += [qraw.at[lax.rem(x + 2, 4), 0:8], qraw.at[lax.rem(x + 2, 4), 8:16]]
    copies = [
        pltpu.make_async_copy(b.at[:, :, columns], to, sem.at[i])
        for i, (b, to) in enumerate(zip(bufs, into))
    ]
    for c in copies:
        c.start()
    return copies


def flash_kernel(half, owner, lengths, info, *rest):
    bufs, rest = rest[:5], rest[5:]
    kv0, kv1 = rest[:2]
    outs, rest = rest[2:6], rest[6:]
    hold, held, qraw, qs, k1, v1, place, count, first, table, sem = rest
    x, core = info[1], info[2]
    copies = load_queries(bufs, x, slice(half * 256, (half + 1) * 256), qraw, sem)
    loads = []
    for side, kv in enumerate((kv0, kv1)):
        rows = pl.ds(side * 2048, 2048)
        parts = ((0, k1.at[rows, 0:HD]), (0, k1.at[rows, HD : 2 * HD]), (HD, v1.at[rows, 0:HD]))
        for part, (column, into) in enumerate(parts):
            loads.append(
                pltpu.make_async_copy(
                    kv.at[:, column : column + HD], into, sem.at[5 + side * 3 + part]
                )
            )
            loads[-1].start()
    v1[:, HD : 2 * HD] = jnp.ones((4096, HD), jnp.bfloat16)
    rank(owner, place, count)
    total = 0
    for k in range(16):
        at = lax.rem(x + k // 4, 4) * 4 + k % 4
        size = blocks_of(lengths[place[at]], core)

        @pl.loop(0, size)
        def _(t, k=k, total=total):
            table[total + t] = k * 4 + t

        total = total + size
    for spare in range(RB):
        table[total + spare] = 0
    for c in copies:
        c.wait()

    @pl.loop(0, total)
    def _(n):
        code = table[n]
        at = lax.rem(x + lax.div(code, 16), 4) * 4 + lax.rem(lax.div(code, 4), 4)
        i, tb = place[at], lax.rem(code, 4)
        base = lax.rem(n, RB) * TB
        for h in range(2):
            rows = pl.ds(pl.multiple_of(h * RB * TB + base, TB), TB)
            scaled = qraw[tb, i, :, h * HD : (h + 1) * HD].astype(jnp.float32) * SCALE
            high = scaled.astype(jnp.bfloat16)
            qs[lax.div(n, RB), rows, 0:HD] = high
            qs[lax.div(n, RB), rows, HD : 2 * HD] = (scaled - high.astype(jnp.float32)).astype(
                jnp.bfloat16
            )

    for c in loads:
        c.wait()
    rows_of = 2 * RB * TB

    @pl.loop(0, lax.div(total + (RB - 1), RB))
    def _(rb):
        q = qs[rb]
        top = jnp.full((rows_of, HD), LOW, jnp.float32)
        acc = jnp.zeros((rows_of, 2 * HD), jnp.float32)
        for j in range(4096 // KB):
            rows = slice(j * KB, (j + 1) * KB)
            s = lax.dot_general(q, k1[rows, :], NT, preferred_element_type=jnp.float32)
            new = jnp.maximum(top, jnp.max(s, axis=1, keepdims=True))
            p = jnp.exp2(s - new[:, 0:1]).astype(jnp.bfloat16)
            fade = jnp.exp2(top - new)
            acc = acc * jnp.concatenate([fade, fade], axis=1) + lax.dot_general(
                p, v1[rows, :], NN, preferred_element_type=jnp.float32
            )
            top = new
        lane = lax.div(lax.broadcasted_iota(jnp.int32, (TB, HD), 1), 16)
        for i in range(RB):
            n = rb * RB + i
            code = table[n]
            d = jnp.where(n < total, lax.div(code, 16), 4)
            block = lax.rem(code, 16)
            rows = pl.ds(pl.multiple_of(block * TB, TB), TB)
            tops, totals = [], []
            for h in range(2):
                r = h * RB * TB + i * TB
                hold[d, rows, h * HD : (h + 1) * HD] = acc[r : r + TB, 0:HD].astype(jnp.bfloat16)
                tops.append(top[r : r + TB, :])
                totals.append(acc[r : r + TB, HD : 2 * HD])
            group = lax.div(block, 8)
            held[d, group] = jnp.where(
                lane == lax.rem(block, 8), packed_stats(tops, totals), held[d, group]
            )

    copies = []
    for d in range(4):
        for group in range(2):
            hold[d, 512:544, group * HD : (group + 1) * HD] = held[d, group].astype(jnp.bfloat16)
        copies.append(pltpu.make_async_copy(hold.at[d], outs[d], sem.at[d]))
        copies[-1].start()
    for c in copies:
        c.wait()


PART = jax.ShapeDtypeStruct((544, 256), jnp.bfloat16)


def flash(half, owner, lengths, info, bufs, kv0, kv1):
    return pl.pallas_call(
        functools.partial(flash_kernel, half),
        out_shape=(PART,) * 4,
        in_specs=[SMEM, SMEM, SMEM] + [ANY] * 7,
        out_specs=(ANY,) * 4,
        scratch_shapes=[
            pltpu.VMEM((5, 544, 256), jnp.bfloat16),
            pltpu.VMEM((5, 2, TB, HD), jnp.float32),
            pltpu.VMEM((4, 16, TB, 256), jnp.bfloat16),
            pltpu.VMEM((64 // RB, 2 * RB * TB, 2 * HD), jnp.bfloat16),
            pltpu.VMEM((4096, 2 * HD), jnp.bfloat16),
            pltpu.VMEM((4096, 2 * HD), jnp.bfloat16),
            pltpu.SMEM((16,), jnp.int32),
            pltpu.SMEM((8,), jnp.int32),
            pltpu.SMEM((8,), jnp.int32),
            pltpu.SMEM((64 + RB,), jnp.int32),
            pltpu.SemaphoreType.DMA((11,)),
        ],
        compiler_params=pltpu.CompilerParams(vmem_limit_bytes=LIMIT),
        cost_estimate=pl.CostEstimate(
            flops=2 * 2 * 4096 * 4096 * 256, bytes_accessed=5 * 2**20, transcendentals=2**24
        ),
        name="flash",
    )(owner, lengths, info, *bufs, kv0, kv1)


def own_kernel(owner, info, *rest):
    bufs, rest = rest[:5], rest[5:]
    okv, out0, out1, qraw, place, count, sem = rest
    x, core = info[1], info[2]
    copies = load_queries(bufs, x, slice(0, 512), qraw, sem)
    rank(owner, place, count)
    held = [[jnp.zeros((TB, HD), jnp.float32) for _ in range(2)] for _ in range(2)]
    lane = lax.div(lax.broadcasted_iota(jnp.int32, (TB, HD), 1), 16)
    for c in copies:
        c.wait()
    row = lax.broadcasted_iota(jnp.int32, (512, 256), 0)
    token = lax.div(lax.rem(row, 128), TB) * (2 * TB) + core * TB + lax.rem(row, TB)
    allowed = lax.broadcasted_iota(jnp.int32, (512, 256), 1) <= token
    for slot in range(4):
        i = place[x * 4 + slot]
        q = jnp.concatenate(
            [qraw[tb, i, :, h * HD : (h + 1) * HD] for h in range(4) for tb in range(4)], axis=0
        )
        base = slot * 256
        keys = jnp.concatenate([okv[t, :, base : base + HD] for t in range(8)], axis=0)
        vals = jnp.concatenate([okv[t, :, base + HD : base + 256] for t in range(8)], axis=0)
        vals = jnp.concatenate([vals, jnp.ones((256, HD), jnp.bfloat16)], axis=1)
        s = lax.dot_general(q, keys, NT, preferred_element_type=jnp.float32) * SCALE
        top = jnp.max(jnp.where(allowed, s, -jnp.inf), axis=1, keepdims=True)
        p = jnp.where(allowed, jnp.exp2(jnp.minimum(s - top, 0.0)), 0.0).astype(jnp.bfloat16)
        acc = lax.dot_general(p, vals, NN, preferred_element_type=jnp.float32)
        top = jnp.broadcast_to(top, (512, HD))
        for half, out in enumerate((out0, out1)):
            for h in range(2):
                r = (half * 2 + h) * 128
                out[slot * 128 : (slot + 1) * 128, h * HD : (h + 1) * HD] = acc[
                    r : r + 128, 0:HD
                ].astype(jnp.bfloat16)
            for tb in range(4):
                block = slot * 4 + tb
                r = [(half * 2 + h) * 128 + tb * TB for h in range(2)]
                st = packed_stats(
                    [top[a : a + TB, :] for a in r], [acc[a : a + TB, HD : 2 * HD] for a in r]
                )
                held[half][block // 8] = jnp.where(lane == block % 8, st, held[half][block // 8])
    for half, out in enumerate((out0, out1)):
        for group in range(2):
            out[512:544, group * HD : (group + 1) * HD] = held[half][group].astype(jnp.bfloat16)


def own_part(owner, info, bufs, okv):
    return pl.pallas_call(
        own_kernel,
        out_shape=(PART,) * 2,
        in_specs=[SMEM, SMEM] + [ANY] * 5 + [VMEM],
        out_specs=(VMEM,) * 2,
        scratch_shapes=[
            pltpu.VMEM((4, 16, TB, 512), jnp.bfloat16),
            pltpu.SMEM((16,), jnp.int32),
            pltpu.SMEM((8,), jnp.int32),
            pltpu.SemaphoreType.DMA((5,)),
        ],
        compiler_params=pltpu.CompilerParams(vmem_limit_bytes=LIMIT),
        cost_estimate=pl.CostEstimate(
            flops=2 * 2 * 2048 * 256 * 256, bytes_accessed=4 * 2**20, transcendentals=2**19
        ),
        name="own_part",
    )(owner, info, *bufs, okv)


def combine_kernel(last, owner, lengths, info, *rest):
    parts, rest = rest[:10], rest[10:]
    if last:
        got, rest = rest[0], rest[1:]
    out, body, tail, place, count, sem = rest
    x, core = info[1], info[2]
    group = core if last else 1 - core
    rows = pl.ds(pl.multiple_of(group * 256, 256), 256)
    columns = pl.ds(pl.multiple_of(group * HD, HD), HD)
    copies = []
    for i, part in enumerate(parts):
        copies.append(pltpu.make_async_copy(part.at[rows, :], body.at[i], sem.at[2 * i]))
        copies.append(
            pltpu.make_async_copy(part.at[512:544, columns], tail.at[i], sem.at[2 * i + 1])
        )
    for c in copies:
        c.start()
    rank(owner, place, count)
    lane = lax.rem(lax.broadcasted_iota(jnp.int32, (HD, 512), 0), 16)
    col = lax.broadcasted_iota(jnp.int32, (HD, 512), 1)
    kind = lax.rem(lane, 8) - 3 * lax.div(col, 256)
    pick = (lax.div(lane, 8) == lax.div(lax.rem(col, 256), HD)) & (kind >= 0) & (kind < 3)
    pick = pick.astype(jnp.float32).astype(jnp.bfloat16)
    block = lax.div(lax.broadcasted_iota(jnp.int32, (TB, HD), 1), 16)
    row = lax.broadcasted_iota(jnp.int32, (128, 1), 0)
    token = lax.div(row, TB) * (2 * TB) + core * TB + lax.rem(row, TB)
    for c in copies:
        c.wait()
    for slot in range(2):
        valid = token < lengths[place[(x * 2 + group) * 2 + slot]]
        for half in range(2):
            wide = []
            for i in range(5):
                st = tail[half * 5 + i].astype(jnp.float32)
                st = jnp.concatenate(
                    [jnp.where(block == slot * 4 + b, st, 0.0) for b in range(4)], axis=0
                )
                wide.append(
                    lax.dot_general(
                        st.astype(jnp.bfloat16), pick, NN, preferred_element_type=jnp.float32
                    )
                )
            top = functools.reduce(jnp.maximum, [w[:, 0:256] for w in wide])
            numer, denom = 0.0, 0.0
            for i, w in enumerate(wide):
                f = jnp.exp2(w[:, 0:256] - top)
                o = body[half * 5 + i, slot * 128 : (slot + 1) * 128, :]
                numer = numer + o.astype(jnp.float32) * f
                denom = denom + w[:, 256:512] * f
            done = jnp.where(valid, numer / denom, 0.0).astype(jnp.bfloat16)
            wide_columns = slice(half * 256, (half + 1) * 256)
            for tb in range(4):
                value = done[tb * TB : (tb + 1) * TB, :]
                if last:
                    mine = pl.ds(pl.multiple_of(slot * 256 + tb * 64 + core * TB, TB), TB)
                    out[mine, wide_columns] = value
                else:
                    out[slot * 128 + tb * TB : slot * 128 + (tb + 1) * TB, wide_columns] = value
    if last:
        for slot in range(2):
            for tb in range(4):
                theirs = pl.ds(pl.multiple_of(slot * 256 + tb * 64 + (1 - core) * TB, TB), TB)
                out[theirs, :] = got[slot * 128 + tb * TB : slot * 128 + (tb + 1) * TB, :]


def combine(last, owner, lengths, info, parts, got=()):
    return pl.pallas_call(
        functools.partial(combine_kernel, last),
        out_shape=jax.ShapeDtypeStruct((512 if last else 256, 512), jnp.bfloat16),
        in_specs=[SMEM, SMEM, SMEM] + [ANY] * 10 + [VMEM] * len(got),
        out_specs=VMEM,
        scratch_shapes=[
            pltpu.VMEM((10, 256, 256), jnp.bfloat16),
            pltpu.VMEM((10, TB, HD), jnp.bfloat16),
            pltpu.SMEM((16,), jnp.int32),
            pltpu.SMEM((8,), jnp.int32),
            pltpu.SemaphoreType.DMA((20,)),
        ],
        compiler_params=pltpu.CompilerParams(vmem_limit_bytes=LIMIT),
        name="combine_own" if last else "combine",
    )(owner, lengths, info, *parts, *got)


def split_kernel(left, right, lower, upper, sem):
    copies = [
        pltpu.make_async_copy(left.at[0:8], lower, sem.at[0]),
        pltpu.make_async_copy(right.at[8:16], upper, sem.at[1]),
    ]
    for c in copies:
        c.start()
    for c in copies:
        c.wait()


def split(left, right):
    return pl.pallas_call(
        split_kernel,
        out_shape=(jax.ShapeDtypeStruct((8, 32, 512), jnp.bfloat16),) * 2,
        in_specs=[ANY, ANY],
        out_specs=(VMEM, VMEM),
        scratch_shapes=[pltpu.SemaphoreType.DMA((2,))],
        compiler_params=pltpu.CompilerParams(vmem_limit_bytes=4 * 2**20),
        cost_estimate=pl.CostEstimate(
            flops=2 * 10**11, bytes_accessed=2**20, transcendentals=0
        ),
        name="split",
    )(left, right)


CORE = [(i, i ^ 1) for i in range(8)]


def along_x(shift):
    return [(i, (i + 2 * shift) % 8) for i in range(8)]


def local(queries, cand_kv, prefix_kv, lengths, owner):
    g = lax.axis_index("group")
    info = jnp.stack([lax.axis_index("prefix") // 2, g // 2, g % 2, g]).astype(jnp.int32)
    swap = lambda a: lax.ppermute(a, "group", CORE)
    left = lax.ppermute(queries, "group", along_x(1))
    right = lax.ppermute(queries, "group", along_x(3))
    kvsend, okvsend = prep(info, owner, cand_kv, prefix_kv)
    kv0 = lax.all_to_all(kvsend, "prefix", split_axis=0, concat_axis=0, tiled=True)
    lower, upper = split(left, right)
    lower = lax.ppermute(lower, "group", along_x(1))
    upper = lax.ppermute(upper, "group", along_x(3))
    kv0, lower, upper = lax.optimization_barrier((kv0, lower, upper))
    kv0 = kv0.reshape(2048, 256)
    kv1 = swap(kv0)
    bufs = [queries, left, right, lower, upper]
    parts = []
    for half in range(2):
        mine, *sent = flash(half, owner, lengths, info, bufs, kv0, kv1)
        parts.append([mine] + [lax.ppermute(o, "group", along_x(s + 1)) for s, o in enumerate(sent)])
        if half == 0:
            okvsend, _ = lax.optimization_barrier((okvsend, kv0))
            okv = lax.all_to_all(okvsend, "group", split_axis=0, concat_axis=0, tiled=True)
    own = own_part(owner, info, bufs, okv)
    parts = [a for half in range(2) for a in parts[half] + [own[half]]]
    got = swap(combine(False, owner, lengths, info, parts))
    return combine(True, owner, lengths, info, parts, (got,)).reshape(2, 256, 512)


def solution(mesh):
    return jax.shard_map(
        local,
        mesh=mesh,
        in_specs=(P(None, "group", "prefix"), P(None, "group", None), P("prefix", None), P(), P()),
        out_specs=P("group", None, "prefix"),
        check_vma=False,
    )
```

```python
import functools
import math

import jax
import jax.numpy as jnp
from jax import lax
from jax.experimental import pallas as pl
from jax.experimental.pallas import tpu as pltpu
from jax.sharding import PartitionSpec as P

H = 64
KVH = 8
HD = 128
NT = (((1,), (1,)), ((), ()))
NN = (((1,), (0,)), ((), ()))
SCALE = math.log2(math.e) / math.sqrt(HD)
LOW = -1e30
LIMIT = 60 * 2**20
VMEM = pl.BlockSpec(memory_space=pltpu.VMEM)
SMEM = pl.BlockSpec(memory_space=pltpu.SMEM)
ANY = pl.BlockSpec(memory_space=pl.ANY)
TB = 32
RB = 16
KB = 256


def prep_kernel(info, kv, kvsend, slab, sem):
    rows = pl.ds(pl.multiple_of(info[3] * HD, HD), HD)
    copy = pltpu.make_async_copy(kv.at[rows, :], slab, sem)
    copy.start()
    copy.wait()
    for dest in range(16):
        for half in range(2):
            column = (half * KVH + dest // 2) * HD
            kvsend[dest, :, half * HD : (half + 1) * HD] = slab[:, column : column + HD]


def prep(info, kv):
    return pl.pallas_call(
        prep_kernel,
        out_shape=jax.ShapeDtypeStruct((16, 128, 256), jnp.bfloat16),
        in_specs=[SMEM, ANY],
        out_specs=VMEM,
        scratch_shapes=[pltpu.VMEM((HD, 2048), jnp.bfloat16), pltpu.SemaphoreType.DMA],
        compiler_params=pltpu.CompilerParams(vmem_limit_bytes=LIMIT),
        name="prep",
    )(info, kv)


def prep_own_kernel(info, owner, cand, okvsend, own, count, sem):
    head = pl.multiple_of(info[0] * HD, HD)
    copies = [
        pltpu.make_async_copy(cand.at[:, :, pl.ds(head, HD)], own.at[:, :, 0:HD], sem.at[0]),
        pltpu.make_async_copy(
            cand.at[:, :, pl.ds(pl.multiple_of(head + KVH * HD, HD), HD)],
            own.at[:, :, HD : 2 * HD],
            sem.at[1],
        ),
    ]
    for copy in copies:
        copy.start()
    for copy in copies:
        copy.wait()
    for o in range(8):
        count[o] = 0
    for i in range(16):
        o = owner[i]
        slot = (o & 1) * 2 + count[o]
        count[o] = count[o] + 1
        for s in range(4):

            @pl.when(slot == s)
            def _(i=i, s=s, x=o >> 1):
                for core in range(2):
                    okvsend[x * 2 + core, :, s * 256 : (s + 1) * 256] = own[i]


def prep_own(info, owner, cand):
    return pl.pallas_call(
        prep_own_kernel,
        out_shape=jax.ShapeDtypeStruct((8, 32, 1024), jnp.bfloat16),
        in_specs=[SMEM, SMEM, ANY],
        out_specs=VMEM,
        scratch_shapes=[
            pltpu.VMEM((16, 32, 256), jnp.bfloat16),
            pltpu.SMEM((8,), jnp.int32),
            pltpu.SemaphoreType.DMA((2,)),
        ],
        compiler_params=pltpu.CompilerParams(vmem_limit_bytes=LIMIT),
        name="prep_own",
    )(info, owner, cand)


def rank(owner, place, count):
    for o in range(8):
        count[o] = 0
    for i in range(16):
        o = owner[i]
        place[o * 2 + count[o]] = i
        count[o] = count[o] + 1


def blocks_of(length, core):
    return (length - TB * core + (2 * TB - 1)) >> 6


def packed_stats(tops, totals):
    lane = lax.broadcasted_iota(jnp.int32, (TB, HD), 1)
    kind = lane & 7
    first, second = (jnp.where(kind < 3, tops[h], totals[h]) for h in range(2))
    value = jnp.where((lane & 8) == 0, first, second)
    hi = value.astype(jnp.bfloat16).astype(jnp.float32)
    mid = (value - hi).astype(jnp.bfloat16).astype(jnp.float32)
    low = jnp.where((kind == 2) | (kind == 5), value - hi - mid, 0.0)
    value = jnp.where((kind == 0) | (kind == 3), hi, low)
    value = jnp.where((kind == 1) | (kind == 4), mid, value)
    return value


def load_queries(bufs, x, columns, qraw, sem):
    into = [qraw.at[(x + shift) & 3] for shift in (0, 3, 1)]
    into += [qraw.at[(x + 2) & 3, 0:8], qraw.at[(x + 2) & 3, 8:16]]
    copies = [
        pltpu.make_async_copy(b.at[:, :, columns], to, sem.at[i])
        for i, (b, to) in enumerate(zip(bufs, into))
    ]
    for c in copies:
        c.start()
    return copies


def flash_kernel(half, owner, lengths, info, *rest):
    bufs, rest = rest[:5], rest[5:]
    kv0, kv1 = rest[:2]
    if half == 1:
        okv, rest = rest[2], rest[3:]
        outs, own_outs, rest = rest[:4], rest[4:6], rest[6:]
    else:
        outs, rest = rest[2:6], rest[6:]
    hold, held, qraw, qs, k1, v1, place, count, table, sem = rest
    x, core = info[1], info[2]
    copies = load_queries(bufs, x, slice(0, 256 + 256 * half), qraw, sem)
    loads = []
    for side, kv in enumerate((kv0, kv1)):
        rows = pl.ds(side * 2048, 2048)
        parts = ((0, k1.at[rows, 0:HD]), (0, k1.at[rows, HD : 2 * HD]), (HD, v1.at[rows, 0:HD]))
        for part, (column, into) in enumerate(parts):
            loads.append(
                pltpu.make_async_copy(
                    kv.at[:, column : column + HD], into, sem.at[5 + side * 3 + part]
                )
            )
            loads[-1].start()
    v1[:, HD : 2 * HD] = jnp.ones((4096, HD), jnp.bfloat16)
    rank(owner, place, count)
    total = 0
    for k in range(16):
        at = ((x + k // 4) & 3) * 4 + k % 4
        size = blocks_of(lengths[place[at]], core)

        @pl.loop(0, size)
        def _(t, k=k, total=total):
            table[total + t] = k * 4 + t

        total = total + size
    for spare in range(2 * RB):
        table[total + spare] = 0
    for c in copies:
        c.wait()

    def gather(first, count, into):
        for i in range(count):
            code = table[first + i]
            at = ((x + (code >> 4)) & 3) * 4 + ((code >> 2) & 3)
            for h in range(2):
                column = half * 256 + h * HD
                block = qraw[code & 3, place[at], :, column : column + HD]
                scaled = block.astype(jnp.float32) * SCALE
                high = scaled.astype(jnp.bfloat16)
                rows = slice((h * count + i) * TB, (h * count + i + 1) * TB)
                qs[into, rows, 0:HD] = high
                qs[into, rows, HD : 2 * HD] = (scaled - high.astype(jnp.float32)).astype(
                    jnp.bfloat16
                )

    gather(0, RB, 0)
    if half == 1:
        own_passages(info, qraw, okv, place, own_outs)
    for c in loads:
        c.wait()
    lane = lax.broadcasted_iota(jnp.int32, (TB, HD), 1) >> 4

    def attend(q, first, count):
        top = jnp.full((2 * count * TB, HD), LOW, jnp.float32)
        acc = jnp.zeros((2 * count * TB, 2 * HD), jnp.float32)
        for j in range(4096 // KB):
            rows = slice(j * KB, (j + 1) * KB)
            s = lax.dot_general(q, k1[rows, :], NT, preferred_element_type=jnp.float32)
            new = jnp.maximum(top, jnp.max(s, axis=1, keepdims=True))
            p = jnp.exp2(s - new[:, 0:1]).astype(jnp.bfloat16)
            fade = jnp.exp2(top - new)
            acc = acc * jnp.concatenate([fade, fade], axis=1) + lax.dot_general(
                p, v1[rows, :], NN, preferred_element_type=jnp.float32
            )
            top = new
        for i in range(count):
            n = first + i
            code = table[n]
            d = jnp.where(n < total, code >> 4, 4)
            block = code & 15
            rows = pl.ds(pl.multiple_of(block * TB, TB), TB)
            tops, totals = [], []
            for h in range(2):
                r = (h * count + i) * TB
                hold[d, rows, h * HD : (h + 1) * HD] = acc[r : r + TB, 0:HD].astype(jnp.bfloat16)
                tops.append(top[r : r + TB, :])
                totals.append(acc[r : r + TB, HD : 2 * HD])
            group = block >> 3
            held[d, group] = jnp.where(
                lane == (block & 7), packed_stats(tops, totals), held[d, group]
            )

    rest_of = total & (RB - 1)
    few = (rest_of > 0) & (rest_of <= RB // 2)
    whole = (total >> 4) + (rest_of > RB // 2).astype(jnp.int32)

    @pl.loop(0, whole)
    def _(rb):
        q = qs[rb & 1]
        gather((rb + 1) * RB, RB, (rb + 1) & 1)
        attend(q, rb * RB, RB)

    @pl.when(few)
    def _():
        gather(whole * RB, RB // 2, 0)
        attend(qs[0, 0 : RB * TB], whole * RB, RB // 2)

    copies = []
    for d in range(4):
        for group in range(2):
            hold[d, 512:544, group * HD : (group + 1) * HD] = held[d, group].astype(jnp.bfloat16)
        copies.append(pltpu.make_async_copy(hold.at[d], outs[d], sem.at[d]))
        copies[-1].start()
    for c in copies:
        c.wait()


def own_passages(info, qraw, okv, place, outs):
    x, core = info[1], info[2]
    held = [[jnp.zeros((TB, HD), jnp.float32) for _ in range(2)] for _ in range(2)]
    lane = lax.broadcasted_iota(jnp.int32, (TB, HD), 1) >> 4
    row = lax.broadcasted_iota(jnp.int32, (512, 256), 0)
    token = ((row & 127) >> 5) * (2 * TB) + core * TB + (row & (TB - 1))
    allowed = lax.broadcasted_iota(jnp.int32, (512, 256), 1) <= token
    for slot in range(4):
        i = place[x * 4 + slot]
        q = jnp.concatenate(
            [qraw[tb, i, :, h * HD : (h + 1) * HD] for h in range(4) for tb in range(4)], axis=0
        )
        base = slot * 256
        keys = jnp.concatenate([okv[t, :, base : base + HD] for t in range(8)], axis=0)
        vals = jnp.concatenate([okv[t, :, base + HD : base + 256] for t in range(8)], axis=0)
        vals = jnp.concatenate([vals, jnp.ones((256, HD), jnp.bfloat16)], axis=1)
        s = lax.dot_general(q, keys, NT, preferred_element_type=jnp.float32) * SCALE
        top = jnp.max(jnp.where(allowed, s, -jnp.inf), axis=1, keepdims=True)
        p = jnp.where(allowed, jnp.exp2(jnp.minimum(s - top, 0.0)), 0.0).astype(jnp.bfloat16)
        acc = lax.dot_general(p, vals, NN, preferred_element_type=jnp.float32)
        top = jnp.broadcast_to(top, (512, HD))
        for half, out in enumerate(outs):
            for h in range(2):
                r = (half * 2 + h) * 128
                out[slot * 128 : (slot + 1) * 128, h * HD : (h + 1) * HD] = acc[
                    r : r + 128, 0:HD
                ].astype(jnp.bfloat16)
            for tb in range(4):
                block = slot * 4 + tb
                r = [(half * 2 + h) * 128 + tb * TB for h in range(2)]
                st = packed_stats(
                    [top[a : a + TB, :] for a in r], [acc[a : a + TB, HD : 2 * HD] for a in r]
                )
                held[half][block // 8] = jnp.where(lane == block % 8, st, held[half][block // 8])
    for half, out in enumerate(outs):
        for group in range(2):
            out[512:544, group * HD : (group + 1) * HD] = held[half][group].astype(jnp.bfloat16)


PART = jax.ShapeDtypeStruct((544, 256), jnp.bfloat16)


def flash(half, owner, lengths, info, bufs, kv0, kv1, okv=None):
    more = half == 1
    return pl.pallas_call(
        functools.partial(flash_kernel, half),
        out_shape=(PART,) * (6 if more else 4),
        in_specs=[SMEM, SMEM, SMEM] + [ANY] * 7 + [VMEM] * more,
        out_specs=(ANY,) * 4 + (VMEM,) * (2 * more),
        scratch_shapes=[
            pltpu.VMEM((5, 544, 256), jnp.bfloat16),
            pltpu.VMEM((5, 2, TB, HD), jnp.float32),
            pltpu.VMEM((4, 16, TB, 512 if more else 256), jnp.bfloat16),
            pltpu.VMEM((2, 2 * RB * TB, 2 * HD), jnp.bfloat16),
            pltpu.VMEM((4096, 2 * HD), jnp.bfloat16),
            pltpu.VMEM((4096, 2 * HD), jnp.bfloat16),
            pltpu.SMEM((16,), jnp.int32),
            pltpu.SMEM((8,), jnp.int32),
            pltpu.SMEM((64 + 2 * RB,), jnp.int32),
            pltpu.SemaphoreType.DMA((11,)),
        ],
        compiler_params=pltpu.CompilerParams(vmem_limit_bytes=LIMIT),
        cost_estimate=pl.CostEstimate(
            flops=2 * 2 * 4096 * 4096 * 256, bytes_accessed=5 * 2**20, transcendentals=2**24
        ),
        name="flash_and_own" if more else "flash",
    )(owner, lengths, info, *bufs, kv0, kv1, *([okv] if more else []))


def combine_kernel(step, owner, lengths, info, *rest):
    parts, rest = rest[:5], rest[5:]
    if step > 0:
        first, rest = rest[0], rest[1:]
    if step == 2:
        got, rest = rest[0], rest[1:]
    out, body, tail, place, count, sem = rest
    x, core = info[1], info[2]
    group = (0, 1 - core, core)[step]
    size = 512 if step == 0 else 256
    rows = pl.ds(pl.multiple_of(group * 256, 256), size)
    columns = pl.ds(pl.multiple_of(group * HD, HD), size // 2)
    copies = []
    for i, part in enumerate(parts):
        copies.append(pltpu.make_async_copy(part.at[rows, :], body.at[i], sem.at[2 * i]))
        copies.append(
            pltpu.make_async_copy(part.at[512:544, columns], tail.at[i], sem.at[2 * i + 1])
        )
    for c in copies:
        c.start()
    rank(owner, place, count)
    lane = lax.broadcasted_iota(jnp.int32, (HD, 512), 0)
    col = lax.broadcasted_iota(jnp.int32, (HD, 512), 1)
    kind = (lane & 7) - 3 * (col >> 8)
    pick = (((lane >> 3) & 1) == ((col >> 7) & 1)) & (kind >= 0) & (kind < 3)
    pick = pick.astype(jnp.float32).astype(jnp.bfloat16)
    block = lax.broadcasted_iota(jnp.int32, (TB, HD), 1) >> 4
    row = lax.broadcasted_iota(jnp.int32, (128, 1), 0)
    token = (row >> 5) * (2 * TB) + core * TB + (row & (TB - 1))

    def target(slot, tb, of):
        return pl.ds(pl.multiple_of(slot * 256 + tb * 64 + of * TB, TB), TB)

    if step == 1:
        out[:, 0:256] = first[rows, :]
    if step == 2:
        for slot in range(2):
            for tb in range(4):
                place_of = pl.ds(pl.multiple_of(group * 256 + slot * 128 + tb * TB, TB), TB)
                out[target(slot, tb, core), 0:256] = first[place_of, :]
                out[target(slot, tb, 1 - core), :] = got[
                    slot * 128 + tb * TB : slot * 128 + (tb + 1) * TB, :
                ]
    for c in copies:
        c.wait()
    for slot in range(size // 128):
        valid = token < lengths[place[(x * 2 + group) * 2 + slot]]
        wide = []
        for i in range(5):
            st = tail[i, :, (slot // 2) * HD : (slot // 2 + 1) * HD].astype(jnp.float32)
            st = jnp.concatenate(
                [jnp.where(block == (slot % 2) * 4 + b, st, 0.0) for b in range(4)], axis=0
            )
            wide.append(
                lax.dot_general(
                    st.astype(jnp.bfloat16), pick, NN, preferred_element_type=jnp.float32
                )
            )
        top = functools.reduce(jnp.maximum, [w[:, 0:256] for w in wide])
        numer, denom = 0.0, 0.0
        for i, w in enumerate(wide):
            f = jnp.exp2(w[:, 0:256] - top)
            numer = numer + body[i, slot * 128 : (slot + 1) * 128, :].astype(jnp.float32) * f
            denom = denom + w[:, 256:512] * f
        done = jnp.where(valid, numer / denom, 0.0).astype(jnp.bfloat16)
        if step == 0:
            out[slot * 128 : (slot + 1) * 128, :] = done
        elif step == 1:
            out[slot * 128 : (slot + 1) * 128, 256:512] = done
        else:
            for tb in range(4):
                out[target(slot, tb, core), 256:512] = done[tb * TB : (tb + 1) * TB, :]


def combine(step, owner, lengths, info, parts, *more):
    size = 512 if step == 0 else 256
    shape = ((512, 256), (256, 512), (512, 512))[step]
    return pl.pallas_call(
        functools.partial(combine_kernel, step),
        out_shape=jax.ShapeDtypeStruct(shape, jnp.bfloat16),
        in_specs=[SMEM, SMEM, SMEM] + [ANY] * 5 + [VMEM] * step,
        out_specs=VMEM,
        scratch_shapes=[
            pltpu.VMEM((5, size, 256), jnp.bfloat16),
            pltpu.VMEM((5, TB, size // 2), jnp.bfloat16),
            pltpu.SMEM((16,), jnp.int32),
            pltpu.SMEM((8,), jnp.int32),
            pltpu.SemaphoreType.DMA((10,)),
        ],
        compiler_params=pltpu.CompilerParams(vmem_limit_bytes=LIMIT),
        name=f"combine_{step}",
    )(owner, lengths, info, *parts, *more)


def split_kernel(left, right, lower, upper, sem):
    copies = [
        pltpu.make_async_copy(left.at[0:8], lower, sem.at[0]),
        pltpu.make_async_copy(right.at[8:16], upper, sem.at[1]),
    ]
    for c in copies:
        c.start()
    for c in copies:
        c.wait()


def split(left, right):
    return pl.pallas_call(
        split_kernel,
        out_shape=(jax.ShapeDtypeStruct((8, 32, 512), jnp.bfloat16),) * 2,
        in_specs=[ANY, ANY],
        out_specs=(VMEM, VMEM),
        scratch_shapes=[pltpu.SemaphoreType.DMA((2,))],
        compiler_params=pltpu.CompilerParams(vmem_limit_bytes=4 * 2**20),
        cost_estimate=pl.CostEstimate(
            flops=2 * 10**11, bytes_accessed=2**20, transcendentals=0
        ),
        name="split",
    )(left, right)


CORE = [(i, i ^ 1) for i in range(8)]


def along_x(shift):
    return [(i, (i + 2 * shift) % 8) for i in range(8)]


def local(queries, cand_kv, prefix_kv, lengths, owner):
    g = lax.axis_index("group")
    info = jnp.stack([lax.axis_index("prefix") // 2, g // 2, g % 2, g]).astype(jnp.int32)
    swap = lambda a: lax.ppermute(a, "group", CORE)
    left = lax.ppermute(queries, "group", along_x(1))
    right = lax.ppermute(queries, "group", along_x(3))
    kvsend = prep(info, prefix_kv)
    kv0 = lax.all_to_all(kvsend, "prefix", split_axis=0, concat_axis=0, tiled=True)
    lower, upper = split(left, right)
    lower = lax.ppermute(lower, "group", along_x(1))
    upper = lax.ppermute(upper, "group", along_x(3))
    kv0, lower, upper = lax.optimization_barrier((kv0, lower, upper))
    kv0 = kv0.reshape(2048, 256)
    kv1 = swap(kv0)
    bufs = [queries, left, right, lower, upper]
    cand_kv, _ = lax.optimization_barrier((cand_kv, left))
    okvsend = prep_own(info, owner, cand_kv)
    okvsend, _ = lax.optimization_barrier((okvsend, kv0))
    okv = lax.all_to_all(okvsend, "group", split_axis=0, concat_axis=0, tiled=True)
    send = lambda outs: [lax.ppermute(o, "group", along_x(s + 1)) for s, o in enumerate(outs)]
    mine0, *sent = flash(0, owner, lengths, info, bufs, kv0, kv1)
    got0 = send(sent)
    mine1, *sent, own0, own1 = flash(1, owner, lengths, info, bufs, kv0, kv1, okv)
    got1 = send(sent)
    first = combine(0, owner, lengths, info, [mine0, *got0, own0])
    first, *got1 = lax.optimization_barrier((first, *got1))
    parts = [mine1, *got1, own1]
    got = swap(combine(1, owner, lengths, info, parts, first))
    return combine(2, owner, lengths, info, parts, first, got).reshape(2, 256, 512)


def solution(mesh):
    return jax.shard_map(
        local,
        mesh=mesh,
        in_specs=(P(None, "group", "prefix"), P(None, "group", None), P("prefix", None), P(), P()),
        out_specs=P("group", None, "prefix"),
        check_vma=False,
    )
```

```python
import functools
import math

import jax
import jax.numpy as jnp
from jax import lax
from jax.experimental import pallas as pl
from jax.experimental.pallas import tpu as pltpu
from jax.sharding import PartitionSpec as P

H = 64
KVH = 8
HD = 128
NT = (((1,), (1,)), ((), ()))
NN = (((1,), (0,)), ((), ()))
SCALE = math.log2(math.e) / math.sqrt(HD)
LOW = -1e30
LIMIT = 60 * 2**20
VMEM = pl.BlockSpec(memory_space=pltpu.VMEM)
SMEM = pl.BlockSpec(memory_space=pltpu.SMEM)
ANY = pl.BlockSpec(memory_space=pl.ANY)
TB = 32
RB = 16
KB = 256


def prep_kernel(info, kv, kvsend, slab, sem):
    rows = pl.ds(pl.multiple_of(info[3] * HD, HD), HD)
    copy = pltpu.make_async_copy(kv.at[rows, :], slab, sem)
    copy.start()
    copy.wait()
    for dest in range(16):
        for half in range(2):
            column = (half * KVH + dest // 2) * HD
            kvsend[dest, :, half * HD : (half + 1) * HD] = slab[:, column : column + HD]


def prep(info, kv):
    return pl.pallas_call(
        prep_kernel,
        out_shape=jax.ShapeDtypeStruct((16, 128, 256), jnp.bfloat16),
        in_specs=[SMEM, ANY],
        out_specs=VMEM,
        scratch_shapes=[pltpu.VMEM((HD, 2048), jnp.bfloat16), pltpu.SemaphoreType.DMA],
        compiler_params=pltpu.CompilerParams(vmem_limit_bytes=LIMIT),
        name="prep",
    )(info, kv)


def rank(owner, place, count):
    for o in range(8):
        count[o] = 0
    for i in range(16):
        o = owner[i]
        place[o * 2 + count[o]] = i
        count[o] = count[o] + 1


def blocks_of(length, core):
    return (length - TB * core + (2 * TB - 1)) >> 6


def packed_stats(tops, totals):
    lane = lax.broadcasted_iota(jnp.int32, (TB, HD), 1)
    kind = lane & 7
    first, second = (jnp.where(kind < 3, tops[h], totals[h]) for h in range(2))
    value = jnp.where((lane & 8) == 0, first, second)
    hi = value.astype(jnp.bfloat16).astype(jnp.float32)
    mid = (value - hi).astype(jnp.bfloat16).astype(jnp.float32)
    low = jnp.where((kind == 2) | (kind == 5), value - hi - mid, 0.0)
    value = jnp.where((kind == 0) | (kind == 3), hi, low)
    value = jnp.where((kind == 1) | (kind == 4), mid, value)
    return value


def load_queries(bufs, x, columns, qraw, sem):
    into = [qraw.at[(x + shift) & 3] for shift in (0, 3, 1)]
    into += [qraw.at[(x + 2) & 3, 0:8], qraw.at[(x + 2) & 3, 8:16]]
    copies = [
        pltpu.make_async_copy(b.at[:, :, columns], to, sem.at[i])
        for i, (b, to) in enumerate(zip(bufs, into))
    ]
    for c in copies:
        c.start()
    return copies


def flash_kernel(half, owner, lengths, info, *rest):
    bufs, rest = rest[:5], rest[5:]
    kv0, kv1 = rest[:2]
    outs, rest = rest[2:6], rest[6:]
    hold, held, qraw, qs, k1, v1, place, count, table, sem = rest
    x, core = info[1], info[2]
    copies = load_queries(bufs, x, slice(half * 256, half * 256 + 256), qraw, sem)
    loads = []
    for side, kv in enumerate((kv0, kv1)):
        rows = pl.ds(side * 2048, 2048)
        parts = ((0, k1.at[rows, 0:HD]), (0, k1.at[rows, HD : 2 * HD]), (HD, v1.at[rows, 0:HD]))
        for part, (column, into) in enumerate(parts):
            loads.append(
                pltpu.make_async_copy(
                    kv.at[:, column : column + HD], into, sem.at[5 + side * 3 + part]
                )
            )
            loads[-1].start()
    v1[:, HD : 2 * HD] = jnp.ones((4096, HD), jnp.bfloat16)
    rank(owner, place, count)
    total = 0
    for k in range(16):
        at = ((x + k // 4) & 3) * 4 + k % 4
        size = blocks_of(lengths[place[at]], core)

        @pl.loop(0, size)
        def _(t, k=k, total=total):
            table[total + t] = k * 4 + t

        total = total + size
    for spare in range(2 * RB):
        table[total + spare] = 0
    for c in copies:
        c.wait()

    def gather(first, count, into):
        for i in range(count):
            code = table[first + i]
            at = ((x + (code >> 4)) & 3) * 4 + ((code >> 2) & 3)
            for h in range(2):
                block = qraw[code & 3, place[at], :, h * HD : (h + 1) * HD]
                scaled = block.astype(jnp.float32) * SCALE
                high = scaled.astype(jnp.bfloat16)
                rows = slice((h * count + i) * TB, (h * count + i + 1) * TB)
                qs[into, rows, 0:HD] = high
                qs[into, rows, HD : 2 * HD] = (scaled - high.astype(jnp.float32)).astype(
                    jnp.bfloat16
                )

    gather(0, RB, 0)
    for c in loads:
        c.wait()
    lane = lax.broadcasted_iota(jnp.int32, (TB, HD), 1) >> 4

    def attend(q, first, count):
        top = jnp.full((2 * count * TB, HD), LOW, jnp.float32)
        acc = jnp.zeros((2 * count * TB, 2 * HD), jnp.float32)
        for j in range(4096 // KB):
            rows = slice(j * KB, (j + 1) * KB)
            s = lax.dot_general(q, k1[rows, :], NT, preferred_element_type=jnp.float32)
            new = jnp.maximum(top, jnp.max(s, axis=1, keepdims=True))
            p = jnp.exp2(s - new[:, 0:1]).astype(jnp.bfloat16)
            fade = jnp.exp2(top - new)
            acc = acc * jnp.concatenate([fade, fade], axis=1) + lax.dot_general(
                p, v1[rows, :], NN, preferred_element_type=jnp.float32
            )
            top = new
        for i in range(count):
            n = first + i
            code = table[n]
            d = jnp.where(n < total, code >> 4, 4)
            block = code & 15
            rows = pl.ds(pl.multiple_of(block * TB, TB), TB)
            tops, totals = [], []
            for h in range(2):
                r = (h * count + i) * TB
                hold[d, rows, h * HD : (h + 1) * HD] = acc[r : r + TB, 0:HD].astype(jnp.bfloat16)
                tops.append(top[r : r + TB, :])
                totals.append(acc[r : r + TB, HD : 2 * HD])
            group = block >> 3
            held[d, group] = jnp.where(
                lane == (block & 7), packed_stats(tops, totals), held[d, group]
            )

    rest_of = total & (RB - 1)
    few = (rest_of > 0) & (rest_of <= RB // 2)
    whole = (total >> 4) + (rest_of > RB // 2).astype(jnp.int32)

    @pl.loop(0, whole)
    def _(rb):
        q = qs[rb & 1]
        gather((rb + 1) * RB, RB, (rb + 1) & 1)
        attend(q, rb * RB, RB)

    @pl.when(few)
    def _():
        gather(whole * RB, RB // 2, 0)
        attend(qs[0, 0 : RB * TB], whole * RB, RB // 2)

    copies = []
    for d in range(4):
        for group in range(2):
            hold[d, 512:544, group * HD : (group + 1) * HD] = held[d, group].astype(jnp.bfloat16)
        copies.append(pltpu.make_async_copy(hold.at[d], outs[d], sem.at[d]))
        copies[-1].start()
    for c in copies:
        c.wait()


PART = jax.ShapeDtypeStruct((544, 256), jnp.bfloat16)


def flash(half, owner, lengths, info, bufs, kv0, kv1):
    return pl.pallas_call(
        functools.partial(flash_kernel, half),
        out_shape=(PART,) * 4,
        in_specs=[SMEM, SMEM, SMEM] + [ANY] * 7,
        out_specs=(ANY,) * 4,
        scratch_shapes=[
            pltpu.VMEM((5, 544, 256), jnp.bfloat16),
            pltpu.VMEM((5, 2, TB, HD), jnp.float32),
            pltpu.VMEM((4, 16, TB, 256), jnp.bfloat16),
            pltpu.VMEM((2, 2 * RB * TB, 2 * HD), jnp.bfloat16),
            pltpu.VMEM((4096, 2 * HD), jnp.bfloat16),
            pltpu.VMEM((4096, 2 * HD), jnp.bfloat16),
            pltpu.SMEM((16,), jnp.int32),
            pltpu.SMEM((8,), jnp.int32),
            pltpu.SMEM((64 + 2 * RB,), jnp.int32),
            pltpu.SemaphoreType.DMA((11,)),
        ],
        compiler_params=pltpu.CompilerParams(vmem_limit_bytes=LIMIT),
        cost_estimate=pl.CostEstimate(
            flops=2 * 2 * 4096 * 4096 * 256, bytes_accessed=5 * 2**20, transcendentals=2**24
        ),
        name="flash",
    )(owner, lengths, info, *bufs, kv0, kv1)


def own_kernel(owner, info, *rest):
    bufs, rest = rest[:5], rest[5:]
    okv, out0, out1, qraw, place, count, sem = rest
    x, core = info[1], info[2]
    copies = load_queries(bufs, x, slice(0, 512), qraw, sem)
    rank(owner, place, count)
    held = [[jnp.zeros((TB, HD), jnp.float32) for _ in range(2)] for _ in range(2)]
    lane = lax.broadcasted_iota(jnp.int32, (TB, HD), 1) >> 4
    for c in copies:
        c.wait()
    row = lax.broadcasted_iota(jnp.int32, (512, 256), 0)
    token = ((row & 127) >> 5) * (2 * TB) + core * TB + (row & (TB - 1))
    allowed = lax.broadcasted_iota(jnp.int32, (512, 256), 1) <= token
    for slot in range(4):
        i = place[x * 4 + slot]
        q = jnp.concatenate(
            [qraw[tb, i, :, h * HD : (h + 1) * HD] for h in range(4) for tb in range(4)], axis=0
        )
        base = slot * 256
        keys = jnp.concatenate([okv[t, :, base : base + HD] for t in range(8)], axis=0)
        vals = jnp.concatenate([okv[t, :, base + HD : base + 256] for t in range(8)], axis=0)
        vals = jnp.concatenate([vals, jnp.ones((256, HD), jnp.bfloat16)], axis=1)
        s = lax.dot_general(q, keys, NT, preferred_element_type=jnp.float32) * SCALE
        top = jnp.max(jnp.where(allowed, s, -jnp.inf), axis=1, keepdims=True)
        p = jnp.where(allowed, jnp.exp2(jnp.minimum(s - top, 0.0)), 0.0).astype(jnp.bfloat16)
        acc = lax.dot_general(p, vals, NN, preferred_element_type=jnp.float32)
        top = jnp.broadcast_to(top, (512, HD))
        for half, out in enumerate((out0, out1)):
            for h in range(2):
                r = (half * 2 + h) * 128
                out[slot * 128 : (slot + 1) * 128, h * HD : (h + 1) * HD] = acc[
                    r : r + 128, 0:HD
                ].astype(jnp.bfloat16)
            for tb in range(4):
                block = slot * 4 + tb
                r = [(half * 2 + h) * 128 + tb * TB for h in range(2)]
                st = packed_stats(
                    [top[a : a + TB, :] for a in r], [acc[a : a + TB, HD : 2 * HD] for a in r]
                )
                held[half][block // 8] = jnp.where(lane == block % 8, st, held[half][block // 8])
    for half, out in enumerate((out0, out1)):
        for group in range(2):
            out[512:544, group * HD : (group + 1) * HD] = held[half][group].astype(jnp.bfloat16)


def own_part(owner, info, bufs, okv):
    return pl.pallas_call(
        own_kernel,
        out_shape=(PART,) * 2,
        in_specs=[SMEM, SMEM] + [ANY] * 5 + [VMEM],
        out_specs=(VMEM,) * 2,
        scratch_shapes=[
            pltpu.VMEM((4, 16, TB, 512), jnp.bfloat16),
            pltpu.SMEM((16,), jnp.int32),
            pltpu.SMEM((8,), jnp.int32),
            pltpu.SemaphoreType.DMA((5,)),
        ],
        compiler_params=pltpu.CompilerParams(vmem_limit_bytes=LIMIT),
        cost_estimate=pl.CostEstimate(
            flops=2 * 2 * 2048 * 256 * 256, bytes_accessed=4 * 2**20, transcendentals=2**19
        ),
        name="own_part",
    )(owner, info, *bufs, okv)


def combine_kernel(step, owner, lengths, info, *rest):
    parts, rest = rest[:5], rest[5:]
    if step > 0:
        first, rest = rest[0], rest[1:]
    if step == 2:
        got, rest = rest[0], rest[1:]
    out, body, tail, place, count, sem = rest
    x, core = info[1], info[2]
    group = (0, 1 - core, core)[step]
    size = 512 if step == 0 else 256
    rows = pl.ds(pl.multiple_of(group * 256, 256), size)
    columns = pl.ds(pl.multiple_of(group * HD, HD), size // 2)
    copies = []
    for i, part in enumerate(parts):
        copies.append(pltpu.make_async_copy(part.at[rows, :], body.at[i], sem.at[2 * i]))
        copies.append(
            pltpu.make_async_copy(part.at[512:544, columns], tail.at[i], sem.at[2 * i + 1])
        )
    for c in copies:
        c.start()
    rank(owner, place, count)
    lane = lax.broadcasted_iota(jnp.int32, (HD, 512), 0)
    col = lax.broadcasted_iota(jnp.int32, (HD, 512), 1)
    kind = (lane & 7) - 3 * (col >> 8)
    pick = (((lane >> 3) & 1) == ((col >> 7) & 1)) & (kind >= 0) & (kind < 3)
    pick = pick.astype(jnp.float32).astype(jnp.bfloat16)
    block = lax.broadcasted_iota(jnp.int32, (TB, HD), 1) >> 4
    row = lax.broadcasted_iota(jnp.int32, (128, 1), 0)
    token = (row >> 5) * (2 * TB) + core * TB + (row & (TB - 1))

    def target(slot, tb, of):
        return pl.ds(pl.multiple_of(slot * 256 + tb * 64 + of * TB, TB), TB)

    if step == 1:
        out[:, 0:256] = first[rows, :]
    if step == 2:
        for slot in range(2):
            for tb in range(4):
                place_of = pl.ds(pl.multiple_of(group * 256 + slot * 128 + tb * TB, TB), TB)
                out[target(slot, tb, core), 0:256] = first[place_of, :]
                out[target(slot, tb, 1 - core), :] = got[
                    slot * 128 + tb * TB : slot * 128 + (tb + 1) * TB, :
                ]
    for c in copies:
        c.wait()
    for slot in range(size // 128):
        valid = token < lengths[place[(x * 2 + group) * 2 + slot]]
        wide = []
        for i in range(5):
            st = tail[i, :, (slot // 2) * HD : (slot // 2 + 1) * HD].astype(jnp.float32)
            st = jnp.concatenate(
                [jnp.where(block == (slot % 2) * 4 + b, st, 0.0) for b in range(4)], axis=0
            )
            wide.append(
                lax.dot_general(
                    st.astype(jnp.bfloat16), pick, NN, preferred_element_type=jnp.float32
                )
            )
        top = functools.reduce(jnp.maximum, [w[:, 0:256] for w in wide])
        numer, denom = 0.0, 0.0
        for i, w in enumerate(wide):
            f = jnp.exp2(w[:, 0:256] - top)
            numer = numer + body[i, slot * 128 : (slot + 1) * 128, :].astype(jnp.float32) * f
            denom = denom + w[:, 256:512] * f
        done = jnp.where(valid, numer / denom, 0.0).astype(jnp.bfloat16)
        if step == 0:
            out[slot * 128 : (slot + 1) * 128, :] = done
        elif step == 1:
            out[slot * 128 : (slot + 1) * 128, 256:512] = done
        else:
            for tb in range(4):
                out[target(slot, tb, core), 256:512] = done[tb * TB : (tb + 1) * TB, :]


def combine(step, owner, lengths, info, parts, *more):
    size = 512 if step == 0 else 256
    shape = ((512, 256), (256, 512), (512, 512))[step]
    return pl.pallas_call(
        functools.partial(combine_kernel, step),
        out_shape=jax.ShapeDtypeStruct(shape, jnp.bfloat16),
        in_specs=[SMEM, SMEM, SMEM] + [ANY] * 5 + [VMEM] * step,
        out_specs=VMEM,
        scratch_shapes=[
            pltpu.VMEM((5, size, 256), jnp.bfloat16),
            pltpu.VMEM((5, TB, size // 2), jnp.bfloat16),
            pltpu.SMEM((16,), jnp.int32),
            pltpu.SMEM((8,), jnp.int32),
            pltpu.SemaphoreType.DMA((10,)),
        ],
        compiler_params=pltpu.CompilerParams(vmem_limit_bytes=LIMIT),
        name=f"combine_{step}",
    )(owner, lengths, info, *parts, *more)


def split_kernel(info, owner, left, right, cand, lower, upper, okvsend, own, count, sem):
    head = pl.multiple_of(info[0] * HD, HD)
    copies = [
        pltpu.make_async_copy(left.at[0:8], lower, sem.at[0]),
        pltpu.make_async_copy(right.at[8:16], upper, sem.at[1]),
        pltpu.make_async_copy(cand.at[:, :, pl.ds(head, HD)], own.at[:, :, 0:HD], sem.at[2]),
        pltpu.make_async_copy(
            cand.at[:, :, pl.ds(pl.multiple_of(head + KVH * HD, HD), HD)],
            own.at[:, :, HD : 2 * HD],
            sem.at[3],
        ),
    ]
    for c in copies:
        c.start()
    for o in range(8):
        count[o] = 0
    for c in copies:
        c.wait()
    for i in range(16):
        o = owner[i]
        slot = (o & 1) * 2 + count[o]
        count[o] = count[o] + 1
        for s in range(4):

            @pl.when(slot == s)
            def _(i=i, s=s, x=o >> 1):
                for core in range(2):
                    okvsend[x * 2 + core, :, s * 256 : (s + 1) * 256] = own[i]


def split(info, owner, left, right, cand):
    return pl.pallas_call(
        split_kernel,
        out_shape=(jax.ShapeDtypeStruct((8, 32, 512), jnp.bfloat16),) * 2
        + (jax.ShapeDtypeStruct((8, 32, 1024), jnp.bfloat16),),
        in_specs=[SMEM, SMEM, ANY, ANY, ANY],
        out_specs=(VMEM,) * 3,
        scratch_shapes=[
            pltpu.VMEM((16, 32, 256), jnp.bfloat16),
            pltpu.SMEM((8,), jnp.int32),
            pltpu.SemaphoreType.DMA((4,)),
        ],
        compiler_params=pltpu.CompilerParams(vmem_limit_bytes=LIMIT),
        cost_estimate=pl.CostEstimate(
            flops=2 * 10**11, bytes_accessed=2**21, transcendentals=0
        ),
        name="split",
    )(info, owner, left, right, cand)


CORE = [(i, i ^ 1) for i in range(8)]


def along_x(shift):
    return [(i, (i + 2 * shift) % 8) for i in range(8)]


def local(queries, cand_kv, prefix_kv, lengths, owner):
    g = lax.axis_index("group")
    info = jnp.stack([lax.axis_index("prefix") // 2, g // 2, g % 2, g]).astype(jnp.int32)
    swap = lambda a: lax.ppermute(a, "group", CORE)
    left = lax.ppermute(queries, "group", along_x(1))
    right = lax.ppermute(queries, "group", along_x(3))
    kvsend = prep(info, prefix_kv)
    kv0 = lax.all_to_all(kvsend, "prefix", split_axis=0, concat_axis=0, tiled=True)
    lower, upper, okvsend = split(info, owner, left, right, cand_kv)
    lower = lax.ppermute(lower, "group", along_x(1))
    upper = lax.ppermute(upper, "group", along_x(3))
    kv0, lower, upper = lax.optimization_barrier((kv0, lower, upper))
    kv0 = kv0.reshape(2048, 256)
    kv1 = swap(kv0)
    bufs = [queries, left, right, lower, upper]
    okvsend, _ = lax.optimization_barrier((okvsend, kv0))
    okv = lax.all_to_all(okvsend, "group", split_axis=0, concat_axis=0, tiled=True)
    send = lambda outs: [lax.ppermute(o, "group", along_x(s + 1)) for s, o in enumerate(outs)]
    mine0, *sent = flash(0, owner, lengths, info, bufs, kv0, kv1)
    got0 = send(sent)
    mine1, *sent = flash(1, owner, lengths, info, bufs, kv0, kv1)
    got1 = send(sent)
    okv, _ = lax.optimization_barrier((okv, mine1))
    own0, own1 = own_part(owner, info, bufs, okv)
    first = combine(0, owner, lengths, info, [mine0, *got0, own0])
    first, *got1 = lax.optimization_barrier((first, *got1))
    parts = [mine1, *got1, own1]
    got = swap(combine(1, owner, lengths, info, parts, first))
    return combine(2, owner, lengths, info, parts, first, got).reshape(2, 256, 512)


def solution(mesh):
    return jax.shard_map(
        local,
        mesh=mesh,
        in_specs=(P(None, "group", "prefix"), P(None, "group", None), P("prefix", None), P(), P()),
        out_specs=P("group", None, "prefix"),
        check_vma=False,
    )
```

```python
import functools
import math

import jax
import jax.numpy as jnp
from jax import lax
from jax.experimental import pallas as pl
from jax.experimental.pallas import tpu as pltpu
from jax.sharding import PartitionSpec as P

H = 64
KVH = 8
HD = 128
NT = (((1,), (1,)), ((), ()))
NN = (((1,), (0,)), ((), ()))
SCALE = math.log2(math.e) / math.sqrt(HD)
LOW = -1e30
LIMIT = 60 * 2**20
HBM = pl.BlockSpec(memory_space=pltpu.HBM)
VMEM = pl.BlockSpec(memory_space=pltpu.VMEM)
SMEM = pl.BlockSpec(memory_space=pltpu.SMEM)
ANY = pl.BlockSpec(memory_space=pl.ANY)
TB = 32
RB = 16
KB = 256


def prep_kernel(info, kv, kvsend, slab, sem):
    rows = pl.ds(pl.multiple_of(info[3] * HD, HD), HD)
    copy = pltpu.make_async_copy(kv.at[rows, :], slab, sem)
    copy.start()
    copy.wait()
    for dest in range(16):
        for half in range(2):
            column = (half * KVH + dest // 2) * HD
            kvsend[dest, :, half * HD : (half + 1) * HD] = slab[:, column : column + HD]


def prep(info, kv):
    return pl.pallas_call(
        prep_kernel,
        out_shape=jax.ShapeDtypeStruct((16, 128, 256), jnp.bfloat16),
        in_specs=[SMEM, ANY],
        out_specs=VMEM,
        scratch_shapes=[pltpu.VMEM((HD, 2048), jnp.bfloat16), pltpu.SemaphoreType.DMA],
        compiler_params=pltpu.CompilerParams(vmem_limit_bytes=LIMIT),
        name="prep",
    )(info, kv)


def rank(owner, place, count):
    for o in range(8):
        count[o] = 0
    for i in range(16):
        o = owner[i]
        place[o * 2 + count[o]] = i
        count[o] = count[o] + 1


def blocks_of(length, core):
    return (length - TB * core + (2 * TB - 1)) >> 6


def packed_stats(tops, totals):
    lane = lax.broadcasted_iota(jnp.int32, (TB, HD), 1)
    kind = lane & 7
    first, second = (jnp.where(kind < 3, tops[h], totals[h]) for h in range(2))
    value = jnp.where((lane & 8) == 0, first, second)
    hi = value.astype(jnp.bfloat16).astype(jnp.float32)
    mid = (value - hi).astype(jnp.bfloat16).astype(jnp.float32)
    low = jnp.where((kind == 2) | (kind == 5), value - hi - mid, 0.0)
    value = jnp.where((kind == 0) | (kind == 3), hi, low)
    value = jnp.where((kind == 1) | (kind == 4), mid, value)
    return value


def load_queries(bufs, x, columns, qraw, sem):
    into = [qraw.at[(x + shift) & 3] for shift in (0, 3, 1)]
    into += [qraw.at[(x + 2) & 3, 0:8], qraw.at[(x + 2) & 3, 8:16]]
    copies = [
        pltpu.make_async_copy(b.at[:, :, columns], to, sem.at[i])
        for i, (b, to) in enumerate(zip(bufs, into))
    ]
    for c in copies:
        c.start()
    return copies


def flash_kernel(half, owner, lengths, info, *rest):
    bufs, rest = rest[:5], rest[5:]
    kv0, kv1 = rest[:2]
    outs, rest = rest[2:6], rest[6:]
    hold, held, qraw, qs, k1, v1, both, place, count, table, sem = rest
    x, core = info[1], info[2]
    copies = load_queries(bufs, x, slice(half * 256, half * 256 + 256), qraw, sem)
    loads = []
    for side, kv in enumerate((kv0, kv1)):
        for part in range(2):
            loads.append(
                pltpu.make_async_copy(
                    kv.at[part * 1024 : (part + 1) * 1024, :],
                    both.at[pl.ds(side * 2048 + part * 1024, 1024), :],
                    sem.at[5 + side * 2 + part],
                )
            )
            loads[-1].start()
    v1[:, HD : 2 * HD] = jnp.ones((4096, HD), jnp.bfloat16)
    rank(owner, place, count)
    total = 0
    for k in range(16):
        at = ((x + k // 4) & 3) * 4 + k % 4
        size = blocks_of(lengths[place[at]], core)

        @pl.loop(0, size)
        def _(t, k=k, total=total):
            table[total + t] = k * 4 + t

        total = total + size
    for spare in range(2 * RB):
        table[total + spare] = 0
    for c in copies:
        c.wait()

    def gather(first, count, into):
        for i in range(count):
            code = table[first + i]
            at = ((x + (code >> 4)) & 3) * 4 + ((code >> 2) & 3)
            for h in range(2):
                block = qraw[code & 3, place[at], :, h * HD : (h + 1) * HD]
                scaled = block.astype(jnp.float32) * SCALE
                high = scaled.astype(jnp.bfloat16)
                rows = slice((h * count + i) * TB, (h * count + i + 1) * TB)
                qs[into, rows, 0:HD] = high
                qs[into, rows, HD : 2 * HD] = (scaled - high.astype(jnp.float32)).astype(
                    jnp.bfloat16
                )

    gather(0, RB, 0)
    for part, c in enumerate(loads):
        c.wait()
        rows = slice(part * 1024, (part + 1) * 1024)
        k1[rows, 0:HD] = both[rows, 0:HD]
        k1[rows, HD : 2 * HD] = both[rows, 0:HD]
        v1[rows, 0:HD] = both[rows, HD : 2 * HD]
    lane = lax.broadcasted_iota(jnp.int32, (TB, HD), 1) >> 4

    def attend(q, first, count):
        top = jnp.full((2 * count * TB, HD), LOW, jnp.float32)
        acc = jnp.zeros((2 * count * TB, 2 * HD), jnp.float32)
        for j in range(4096 // KB):
            rows = slice(j * KB, (j + 1) * KB)
            s = lax.dot_general(q, k1[rows, :], NT, preferred_element_type=jnp.float32)
            new = jnp.maximum(top, jnp.max(s, axis=1, keepdims=True))
            p = jnp.exp2(s - new[:, 0:1]).astype(jnp.bfloat16)
            fade = jnp.exp2(top - new)
            acc = acc * jnp.concatenate([fade, fade], axis=1) + lax.dot_general(
                p, v1[rows, :], NN, preferred_element_type=jnp.float32
            )
            top = new
        for i in range(count):
            n = first + i
            code = table[n]
            d = jnp.where(n < total, code >> 4, 4)
            block = code & 15
            rows = pl.ds(pl.multiple_of(block * TB, TB), TB)
            tops, totals = [], []
            for h in range(2):
                r = (h * count + i) * TB
                hold[d, rows, h * HD : (h + 1) * HD] = acc[r : r + TB, 0:HD].astype(jnp.bfloat16)
                tops.append(top[r : r + TB, :])
                totals.append(acc[r : r + TB, HD : 2 * HD])
            group = block >> 3
            held[d, group] = jnp.where(
                lane == (block & 7), packed_stats(tops, totals), held[d, group]
            )

    rest_of = total & (RB - 1)
    few = (rest_of > 0) & (rest_of <= RB // 2)
    whole = (total >> 4) + (rest_of > RB // 2).astype(jnp.int32)

    @pl.loop(0, whole)
    def _(rb):
        q = qs[rb & 1]
        gather((rb + 1) * RB, RB, (rb + 1) & 1)
        attend(q, rb * RB, RB)

    @pl.when(few)
    def _():
        gather(whole * RB, RB // 2, 0)
        attend(qs[0, 0 : RB * TB], whole * RB, RB // 2)

    copies = []
    for d in range(4):
        for group in range(2):
            hold[d, 512:544, group * HD : (group + 1) * HD] = held[d, group].astype(jnp.bfloat16)
        copies.append(pltpu.make_async_copy(hold.at[d], outs[d], sem.at[d]))
        copies[-1].start()
    for c in copies:
        c.wait()


PART = jax.ShapeDtypeStruct((544, 256), jnp.bfloat16)


def flash(half, owner, lengths, info, bufs, kv0, kv1):
    return pl.pallas_call(
        functools.partial(flash_kernel, half),
        out_shape=(PART,) * 4,
        in_specs=[SMEM, SMEM, SMEM] + [ANY] * 7,
        out_specs=(ANY,) * 4,
        scratch_shapes=[
            pltpu.VMEM((5, 544, 256), jnp.bfloat16),
            pltpu.VMEM((5, 2, TB, HD), jnp.float32),
            pltpu.VMEM((4, 16, TB, 256), jnp.bfloat16),
            pltpu.VMEM((2, 2 * RB * TB, 2 * HD), jnp.bfloat16),
            pltpu.VMEM((4096, 2 * HD), jnp.bfloat16),
            pltpu.VMEM((4096, 2 * HD), jnp.bfloat16),
            pltpu.VMEM((4096, 2 * HD), jnp.bfloat16),
            pltpu.SMEM((16,), jnp.int32),
            pltpu.SMEM((8,), jnp.int32),
            pltpu.SMEM((64 + 2 * RB,), jnp.int32),
            pltpu.SemaphoreType.DMA((11,)),
        ],
        compiler_params=pltpu.CompilerParams(vmem_limit_bytes=LIMIT),
        cost_estimate=pl.CostEstimate(
            flops=2 * 2 * 4096 * 4096 * 256, bytes_accessed=5 * 2**20, transcendentals=2**24
        ),
        name="flash",
    )(owner, lengths, info, *bufs, kv0, kv1)


def own_kernel(owner, info, *rest):
    bufs, rest = rest[:5], rest[5:]
    okv, out0, out1, qraw, place, count, sem = rest
    x, core = info[1], info[2]
    rank(owner, place, count)
    copies = []
    for slot in range(4):
        i = place[x * 4 + slot]
        for b in range(4):
            into, done = qraw.at[(x + (0, 3, 1, 2)[b]) & 3, slot], sem.at[slot * 4 + b]
            if b < 3:
                copies.append(pltpu.make_async_copy(bufs[b].at[i], into, done))
                copies[-1].start()
            else:
                lower = pltpu.make_async_copy(bufs[3].at[i & 7], into, done)
                upper = pltpu.make_async_copy(bufs[4].at[i & 7], into, done)
                pl.when(i < 8)(lower.start)
                pl.when(i >= 8)(upper.start)
                copies.append(lower)
    held = [[jnp.zeros((TB, HD), jnp.float32) for _ in range(2)] for _ in range(2)]
    lane = lax.broadcasted_iota(jnp.int32, (TB, HD), 1) >> 4
    for c in copies:
        c.wait()
    row = lax.broadcasted_iota(jnp.int32, (512, 256), 0)
    token = ((row & 127) >> 5) * (2 * TB) + core * TB + (row & (TB - 1))
    allowed = lax.broadcasted_iota(jnp.int32, (512, 256), 1) <= token
    for slot in range(4):
        q = jnp.concatenate(
            [qraw[tb, slot, :, h * HD : (h + 1) * HD] for h in range(4) for tb in range(4)], axis=0
        )
        base = slot * 256
        keys = jnp.concatenate([okv[t, :, base : base + HD] for t in range(8)], axis=0)
        vals = jnp.concatenate([okv[t, :, base + HD : base + 256] for t in range(8)], axis=0)
        vals = jnp.concatenate([vals, jnp.ones((256, HD), jnp.bfloat16)], axis=1)
        s = lax.dot_general(q, keys, NT, preferred_element_type=jnp.float32) * SCALE
        top = jnp.max(jnp.where(allowed, s, -jnp.inf), axis=1, keepdims=True)
        p = jnp.where(allowed, jnp.exp2(jnp.minimum(s - top, 0.0)), 0.0).astype(jnp.bfloat16)
        acc = lax.dot_general(p, vals, NN, preferred_element_type=jnp.float32)
        top = jnp.broadcast_to(top, (512, HD))
        for half, out in enumerate((out0, out1)):
            for h in range(2):
                r = (half * 2 + h) * 128
                out[slot * 128 : (slot + 1) * 128, h * HD : (h + 1) * HD] = acc[
                    r : r + 128, 0:HD
                ].astype(jnp.bfloat16)
            for tb in range(4):
                block = slot * 4 + tb
                r = [(half * 2 + h) * 128 + tb * TB for h in range(2)]
                st = packed_stats(
                    [top[a : a + TB, :] for a in r], [acc[a : a + TB, HD : 2 * HD] for a in r]
                )
                held[half][block // 8] = jnp.where(lane == block % 8, st, held[half][block // 8])
    for half, out in enumerate((out0, out1)):
        for group in range(2):
            out[512:544, group * HD : (group + 1) * HD] = held[half][group].astype(jnp.bfloat16)


def own_part(owner, info, bufs, okv):
    return pl.pallas_call(
        own_kernel,
        out_shape=(PART,) * 2,
        in_specs=[SMEM, SMEM] + [HBM] * 5 + [VMEM],
        out_specs=(VMEM,) * 2,
        scratch_shapes=[
            pltpu.VMEM((4, 4, TB, 512), jnp.bfloat16),
            pltpu.SMEM((16,), jnp.int32),
            pltpu.SMEM((8,), jnp.int32),
            pltpu.SemaphoreType.DMA((16,)),
        ],
        compiler_params=pltpu.CompilerParams(vmem_limit_bytes=16 * 2**20),
        cost_estimate=pl.CostEstimate(
            flops=2 * 2 * 2048 * 256 * 256, bytes_accessed=4 * 2**20, transcendentals=2**19
        ),
        name="own_part",
    )(owner, info, *bufs, okv)


def combine_kernel(step, owner, lengths, info, *rest):
    parts, rest = rest[:5], rest[5:]
    if step > 0:
        first, rest = rest[0], rest[1:]
    if step == 2:
        got, rest = rest[0], rest[1:]
    out, body, tail, place, count, sem = rest
    x, core = info[1], info[2]
    group = (0, 1 - core, core)[step]
    size = 512 if step == 0 else 256
    rows = pl.ds(pl.multiple_of(group * 256, 256), size)
    columns = pl.ds(pl.multiple_of(group * HD, HD), size // 2)
    copies = []
    for i, part in enumerate(parts):
        copies.append(pltpu.make_async_copy(part.at[rows, :], body.at[i], sem.at[2 * i]))
        copies.append(
            pltpu.make_async_copy(part.at[512:544, columns], tail.at[i], sem.at[2 * i + 1])
        )
    for c in copies:
        c.start()
    rank(owner, place, count)
    lane = lax.broadcasted_iota(jnp.int32, (HD, 512), 0)
    col = lax.broadcasted_iota(jnp.int32, (HD, 512), 1)
    kind = (lane & 7) - 3 * (col >> 8)
    pick = (((lane >> 3) & 1) == ((col >> 7) & 1)) & (kind >= 0) & (kind < 3)
    pick = pick.astype(jnp.float32).astype(jnp.bfloat16)
    block = lax.broadcasted_iota(jnp.int32, (TB, HD), 1) >> 4
    row = lax.broadcasted_iota(jnp.int32, (128, 1), 0)
    token = (row >> 5) * (2 * TB) + core * TB + (row & (TB - 1))

    def target(slot, tb, of):
        return pl.ds(pl.multiple_of(slot * 256 + tb * 64 + of * TB, TB), TB)

    if step == 1:
        out[:, 0:256] = first[rows, :]
    if step == 2:
        for slot in range(2):
            for tb in range(4):
                place_of = pl.ds(pl.multiple_of(group * 256 + slot * 128 + tb * TB, TB), TB)
                out[target(slot, tb, core), 0:256] = first[place_of, :]
                out[target(slot, tb, 1 - core), :] = got[
                    slot * 128 + tb * TB : slot * 128 + (tb + 1) * TB, :
                ]
    for c in copies:
        c.wait()
    for slot in range(size // 128):
        valid = token < lengths[place[(x * 2 + group) * 2 + slot]]
        wide = []
        for i in range(5):
            st = tail[i, :, (slot // 2) * HD : (slot // 2 + 1) * HD].astype(jnp.float32)
            st = jnp.concatenate(
                [jnp.where(block == (slot % 2) * 4 + b, st, 0.0) for b in range(4)], axis=0
            )
            wide.append(
                lax.dot_general(
                    st.astype(jnp.bfloat16), pick, NN, preferred_element_type=jnp.float32
                )
            )
        top = functools.reduce(jnp.maximum, [w[:, 0:256] for w in wide])
        numer, denom = 0.0, 0.0
        for i, w in enumerate(wide):
            f = jnp.exp2(w[:, 0:256] - top)
            numer = numer + body[i, slot * 128 : (slot + 1) * 128, :].astype(jnp.float32) * f
            denom = denom + w[:, 256:512] * f
        done = jnp.where(valid, numer / denom, 0.0).astype(jnp.bfloat16)
        if step == 0:
            out[slot * 128 : (slot + 1) * 128, :] = done
        elif step == 1:
            out[slot * 128 : (slot + 1) * 128, 256:512] = done
        else:
            for tb in range(4):
                out[target(slot, tb, core), 256:512] = done[tb * TB : (tb + 1) * TB, :]


def combine(step, owner, lengths, info, parts, *more):
    size = 512 if step == 0 else 256
    shape = ((512, 256), (256, 512), (512, 512))[step]
    return pl.pallas_call(
        functools.partial(combine_kernel, step),
        out_shape=jax.ShapeDtypeStruct(shape, jnp.bfloat16),
        in_specs=[SMEM, SMEM, SMEM] + [ANY] * 5 + [VMEM] * step,
        out_specs=VMEM,
        scratch_shapes=[
            pltpu.VMEM((5, size, 256), jnp.bfloat16),
            pltpu.VMEM((5, TB, size // 2), jnp.bfloat16),
            pltpu.SMEM((16,), jnp.int32),
            pltpu.SMEM((8,), jnp.int32),
            pltpu.SemaphoreType.DMA((10,)),
        ],
        compiler_params=pltpu.CompilerParams(vmem_limit_bytes=12 * 2**20),
        name=f"combine_{step}",
    )(owner, lengths, info, *parts, *more)


def split_kernel(info, owner, left, right, cand, lower, upper, okvsend, own, count, sem):
    head = pl.multiple_of(info[0] * HD, HD)
    copies = [
        pltpu.make_async_copy(left.at[0:8], lower, sem.at[0]),
        pltpu.make_async_copy(right.at[8:16], upper, sem.at[1]),
        pltpu.make_async_copy(cand.at[:, :, pl.ds(head, HD)], own.at[:, :, 0:HD], sem.at[2]),
        pltpu.make_async_copy(
            cand.at[:, :, pl.ds(pl.multiple_of(head + KVH * HD, HD), HD)],
            own.at[:, :, HD : 2 * HD],
            sem.at[3],
        ),
    ]
    for c in copies:
        c.start()
    for o in range(8):
        count[o] = 0
    for c in copies:
        c.wait()
    for i in range(16):
        o = owner[i]
        slot = (o & 1) * 2 + count[o]
        count[o] = count[o] + 1
        for s in range(4):

            @pl.when(slot == s)
            def _(i=i, s=s, x=o >> 1):
                for core in range(2):
                    okvsend[x * 2 + core, :, s * 256 : (s + 1) * 256] = own[i]


def split(info, owner, left, right, cand):
    return pl.pallas_call(
        split_kernel,
        out_shape=(jax.ShapeDtypeStruct((8, 32, 512), jnp.bfloat16),) * 2
        + (jax.ShapeDtypeStruct((8, 32, 1024), jnp.bfloat16),),
        in_specs=[SMEM, SMEM, ANY, ANY, ANY],
        out_specs=(VMEM,) * 3,
        scratch_shapes=[
            pltpu.VMEM((16, 32, 256), jnp.bfloat16),
            pltpu.SMEM((8,), jnp.int32),
            pltpu.SemaphoreType.DMA((4,)),
        ],
        compiler_params=pltpu.CompilerParams(vmem_limit_bytes=LIMIT),
        cost_estimate=pl.CostEstimate(
            flops=2 * 10**11, bytes_accessed=2**21, transcendentals=0
        ),
        name="split",
    )(info, owner, left, right, cand)


CORE = [(i, i ^ 1) for i in range(8)]


def along_x(shift):
    return [(i, (i + 2 * shift) % 8) for i in range(8)]


def local(queries, cand_kv, prefix_kv, lengths, owner):
    g = lax.axis_index("group")
    info = jnp.stack([lax.axis_index("prefix") // 2, g // 2, g % 2, g]).astype(jnp.int32)
    swap = lambda a: lax.ppermute(a, "group", CORE)
    left = lax.ppermute(queries, "group", along_x(1))
    right = lax.ppermute(queries, "group", along_x(3))
    kvsend = prep(info, prefix_kv)
    kv0 = lax.all_to_all(kvsend, "prefix", split_axis=0, concat_axis=0, tiled=True)
    lower, upper, okvsend = split(info, owner, left, right, cand_kv)
    lower = lax.ppermute(lower, "group", along_x(1))
    upper = lax.ppermute(upper, "group", along_x(3))
    kv0, lower, upper = lax.optimization_barrier((kv0, lower, upper))
    kv0 = kv0.reshape(2048, 256)
    kv1 = swap(kv0)
    bufs = [queries, left, right, lower, upper]
    okvsend, _ = lax.optimization_barrier((okvsend, kv0))
    okv = lax.all_to_all(okvsend, "group", split_axis=0, concat_axis=0, tiled=True)
    send = lambda outs: [lax.ppermute(o, "group", along_x(s + 1)) for s, o in enumerate(outs)]
    mine0, *sent = flash(0, owner, lengths, info, bufs, kv0, kv1)
    got0 = send(sent)
    mine1, *sent = flash(1, owner, lengths, info, bufs, kv0, kv1)
    got1 = send(sent)
    okv, _ = lax.optimization_barrier((okv, mine1))
    own0, own1 = own_part(owner, info, bufs, okv)
    first = combine(0, owner, lengths, info, [mine0, *got0, own0])
    first, *got1 = lax.optimization_barrier((first, *got1))
    parts = [mine1, *got1, own1]
    got = swap(combine(1, owner, lengths, info, parts, first))
    return combine(2, owner, lengths, info, parts, first, got).reshape(2, 256, 512)


def solution(mesh):
    return jax.shard_map(
        local,
        mesh=mesh,
        in_specs=(P(None, "group", "prefix"), P(None, "group", None), P("prefix", None), P(), P()),
        out_specs=P("group", None, "prefix"),
        check_vma=False,
    )
```

```python
import functools
import math

import jax
import jax.numpy as jnp
from jax import lax
from jax.experimental import pallas as pl
from jax.experimental.pallas import tpu as pltpu
from jax.sharding import PartitionSpec as P

H = 64
KVH = 8
HD = 128
NT = (((1,), (1,)), ((), ()))
NN = (((1,), (0,)), ((), ()))
SCALE = math.log2(math.e) / math.sqrt(HD)
LOW = -1e30
LIMIT = 60 * 2**20
HBM = pl.BlockSpec(memory_space=pltpu.HBM)
VMEM = pl.BlockSpec(memory_space=pltpu.VMEM)
SMEM = pl.BlockSpec(memory_space=pltpu.SMEM)
ANY = pl.BlockSpec(memory_space=pl.ANY)
TB = 32
RB = 16
KB = 256


def prep_kernel(info, kv, kvsend, slab, sem):
    rows = pl.ds(pl.multiple_of(info[3] * HD, HD), HD)
    copy = pltpu.make_async_copy(kv.at[rows, :], slab, sem)
    copy.start()
    copy.wait()
    for dest in range(16):
        for half in range(2):
            column = (half * KVH + dest // 2) * HD
            kvsend[dest, :, half * HD : (half + 1) * HD] = slab[:, column : column + HD]


def prep(info, kv):
    return pl.pallas_call(
        prep_kernel,
        out_shape=jax.ShapeDtypeStruct((16, 128, 256), jnp.bfloat16),
        in_specs=[SMEM, ANY],
        out_specs=VMEM,
        scratch_shapes=[pltpu.VMEM((HD, 2048), jnp.bfloat16), pltpu.SemaphoreType.DMA],
        compiler_params=pltpu.CompilerParams(vmem_limit_bytes=LIMIT),
        name="prep",
    )(info, kv)


def rank(owner, place, count):
    for o in range(8):
        count[o] = 0
    for i in range(16):
        o = owner[i]
        place[o * 2 + count[o]] = i
        count[o] = count[o] + 1


def blocks_of(length, core):
    return (length - TB * core + (2 * TB - 1)) >> 6


def packed_stats(tops, totals):
    lane = lax.broadcasted_iota(jnp.int32, (TB, HD), 1)
    kind = lane & 7
    first, second = (jnp.where(kind < 3, tops[h], totals[h]) for h in range(2))
    value = jnp.where((lane & 8) == 0, first, second)
    hi = value.astype(jnp.bfloat16).astype(jnp.float32)
    mid = (value - hi).astype(jnp.bfloat16).astype(jnp.float32)
    low = jnp.where((kind == 2) | (kind == 5), value - hi - mid, 0.0)
    value = jnp.where((kind == 0) | (kind == 3), hi, low)
    value = jnp.where((kind == 1) | (kind == 4), mid, value)
    return value


def load_queries(bufs, x, columns, qraw, sem):
    into = [qraw.at[(x + shift) & 3] for shift in (0, 3, 1)]
    into += [qraw.at[(x + 2) & 3, 0:8], qraw.at[(x + 2) & 3, 8:16]]
    copies = [
        pltpu.make_async_copy(b.at[:, :, columns], to, sem.at[i])
        for i, (b, to) in enumerate(zip(bufs, into))
    ]
    for c in copies:
        c.start()
    return copies


def flash_kernel(half, owner, lengths, info, *rest):
    bufs, rest = rest[:5], rest[5:]
    kv0, kv1 = rest[:2]
    outs, rest = rest[2:6], rest[6:]
    hold, held, qraw, qs, k1, v1, both, place, count, table, sem = rest
    x, core = info[1], info[2]
    copies = load_queries(bufs, x, slice(half * 256, half * 256 + 256), qraw, sem)
    loads = []
    for side, kv in enumerate((kv0, kv1)):
        for part in range(2):
            loads.append(
                pltpu.make_async_copy(
                    kv.at[part * 1024 : (part + 1) * 1024, :],
                    both.at[pl.ds(side * 2048 + part * 1024, 1024), :],
                    sem.at[5 + side * 2 + part],
                )
            )
            loads[-1].start()
    v1[:, HD : 2 * HD] = jnp.ones((4096, HD), jnp.bfloat16)
    rank(owner, place, count)
    total = 0
    for k in range(16):
        at = ((x + k // 4) & 3) * 4 + k % 4
        size = blocks_of(lengths[place[at]], core)

        @pl.loop(0, size)
        def _(t, k=k, total=total):
            table[total + t] = k * 4 + t

        total = total + size
    for spare in range(2 * RB):
        table[total + spare] = 0
    for c in copies:
        c.wait()

    def gather(first, count, into):
        for i in range(count):
            code = table[first + i]
            at = ((x + (code >> 4)) & 3) * 4 + ((code >> 2) & 3)
            for h in range(2):
                block = qraw[code & 3, place[at], :, h * HD : (h + 1) * HD]
                scaled = block.astype(jnp.float32) * SCALE
                high = scaled.astype(jnp.bfloat16)
                rows = slice((h * count + i) * TB, (h * count + i + 1) * TB)
                qs[into, rows, 0:HD] = high
                qs[into, rows, HD : 2 * HD] = (scaled - high.astype(jnp.float32)).astype(
                    jnp.bfloat16
                )

    gather(0, RB, 0)
    for part, c in enumerate(loads):
        c.wait()
        rows = slice(part * 1024, (part + 1) * 1024)
        k1[rows, 0:HD] = both[rows, 0:HD]
        k1[rows, HD : 2 * HD] = both[rows, 0:HD]
        v1[rows, 0:HD] = both[rows, HD : 2 * HD]
    lane = lax.broadcasted_iota(jnp.int32, (TB, HD), 1) >> 4

    def attend(q, first, count):
        top = jnp.full((2 * count * TB, HD), LOW, jnp.float32)
        acc = jnp.zeros((2 * count * TB, 2 * HD), jnp.float32)
        for j in range(4096 // KB):
            rows = slice(j * KB, (j + 1) * KB)
            s = lax.dot_general(q, k1[rows, :], NT, preferred_element_type=jnp.float32)
            new = jnp.maximum(top, jnp.max(s, axis=1, keepdims=True))
            p = jnp.exp2(s - new[:, 0:1]).astype(jnp.bfloat16)
            fade = jnp.exp2(top - new)
            acc = acc * jnp.concatenate([fade, fade], axis=1) + lax.dot_general(
                p, v1[rows, :], NN, preferred_element_type=jnp.float32
            )
            top = new
        for i in range(count):
            n = first + i
            code = table[n]
            d = jnp.where(n < total, code >> 4, 4)
            block = code & 15
            rows = pl.ds(pl.multiple_of(block * TB, TB), TB)
            tops, totals = [], []
            for h in range(2):
                r = (h * count + i) * TB
                hold[d, rows, h * HD : (h + 1) * HD] = acc[r : r + TB, 0:HD].astype(jnp.bfloat16)
                tops.append(top[r : r + TB, :])
                totals.append(acc[r : r + TB, HD : 2 * HD])
            group = block >> 3
            held[d, group] = jnp.where(
                lane == (block & 7), packed_stats(tops, totals), held[d, group]
            )

    rest_of = total & (RB - 1)
    few = (rest_of > 0) & (rest_of <= RB // 2)
    whole = (total >> 4) + (rest_of > RB // 2).astype(jnp.int32)

    @pl.loop(0, whole)
    def _(rb):
        q = qs[rb & 1]
        gather((rb + 1) * RB, RB, (rb + 1) & 1)
        attend(q, rb * RB, RB)

    @pl.when(few)
    def _():
        gather(whole * RB, RB // 2, 0)
        attend(qs[0, 0 : RB * TB], whole * RB, RB // 2)

    copies = []
    for d in range(4):
        for group in range(2):
            hold[d, 512:544, group * HD : (group + 1) * HD] = held[d, group].astype(jnp.bfloat16)
        copies.append(pltpu.make_async_copy(hold.at[d], outs[d], sem.at[d]))
        copies[-1].start()
    for c in copies:
        c.wait()


PART = jax.ShapeDtypeStruct((544, 256), jnp.bfloat16)


def flash(half, owner, lengths, info, bufs, kv0, kv1):
    return pl.pallas_call(
        functools.partial(flash_kernel, half),
        out_shape=(PART,) * 4,
        in_specs=[SMEM, SMEM, SMEM] + [ANY] * 7,
        out_specs=(ANY,) * 4,
        scratch_shapes=[
            pltpu.VMEM((5, 544, 256), jnp.bfloat16),
            pltpu.VMEM((5, 2, TB, HD), jnp.float32),
            pltpu.VMEM((4, 16, TB, 256), jnp.bfloat16),
            pltpu.VMEM((2, 2 * RB * TB, 2 * HD), jnp.bfloat16),
            pltpu.VMEM((4096, 2 * HD), jnp.bfloat16),
            pltpu.VMEM((4096, 2 * HD), jnp.bfloat16),
            pltpu.VMEM((4096, 2 * HD), jnp.bfloat16),
            pltpu.SMEM((16,), jnp.int32),
            pltpu.SMEM((8,), jnp.int32),
            pltpu.SMEM((64 + 2 * RB,), jnp.int32),
            pltpu.SemaphoreType.DMA((11,)),
        ],
        compiler_params=pltpu.CompilerParams(vmem_limit_bytes=LIMIT),
        cost_estimate=pl.CostEstimate(
            flops=2 * 2 * 4096 * 4096 * 256, bytes_accessed=5 * 2**20, transcendentals=2**24
        ),
        name="flash",
    )(owner, lengths, info, *bufs, kv0, kv1)


def own_kernel(owner, info, *rest):
    bufs, rest = rest[:5], rest[5:]
    okv, out0, out1, qraw, place, count, sem = rest
    x, core = info[1], info[2]
    rank(owner, place, count)
    copies = []
    for slot in range(4):
        i = place[x * 4 + slot]
        for b in range(4):
            into, done = qraw.at[(x + (0, 3, 1, 2)[b]) & 3, slot], sem.at[slot * 4 + b]
            if b < 3:
                copies.append(pltpu.make_async_copy(bufs[b].at[i], into, done))
                copies[-1].start()
            else:
                lower = pltpu.make_async_copy(bufs[3].at[i & 7], into, done)
                upper = pltpu.make_async_copy(bufs[4].at[i & 7], into, done)
                pl.when(i < 8)(lower.start)
                pl.when(i >= 8)(upper.start)
                copies.append(lower)
    held = [[jnp.zeros((TB, HD), jnp.float32) for _ in range(2)] for _ in range(2)]
    lane = lax.broadcasted_iota(jnp.int32, (TB, HD), 1) >> 4
    for c in copies:
        c.wait()
    row = lax.broadcasted_iota(jnp.int32, (512, 256), 0)
    token = ((row & 127) >> 5) * (2 * TB) + core * TB + (row & (TB - 1))
    allowed = lax.broadcasted_iota(jnp.int32, (512, 256), 1) <= token
    for slot in range(4):
        q = jnp.concatenate(
            [qraw[tb, slot, :, h * HD : (h + 1) * HD] for h in range(4) for tb in range(4)], axis=0
        )
        base = slot * 256
        keys = jnp.concatenate([okv[t, :, base : base + HD] for t in range(8)], axis=0)
        vals = jnp.concatenate([okv[t, :, base + HD : base + 256] for t in range(8)], axis=0)
        vals = jnp.concatenate([vals, jnp.ones((256, HD), jnp.bfloat16)], axis=1)
        s = lax.dot_general(q, keys, NT, preferred_element_type=jnp.float32) * SCALE
        top = jnp.max(jnp.where(allowed, s, -jnp.inf), axis=1, keepdims=True)
        p = jnp.where(allowed, jnp.exp2(jnp.minimum(s - top, 0.0)), 0.0).astype(jnp.bfloat16)
        acc = lax.dot_general(p, vals, NN, preferred_element_type=jnp.float32)
        top = jnp.broadcast_to(top, (512, HD))
        for half, out in enumerate((out0, out1)):
            for h in range(2):
                r = (half * 2 + h) * 128
                out[slot * 128 : (slot + 1) * 128, h * HD : (h + 1) * HD] = acc[
                    r : r + 128, 0:HD
                ].astype(jnp.bfloat16)
            for tb in range(4):
                block = slot * 4 + tb
                r = [(half * 2 + h) * 128 + tb * TB for h in range(2)]
                st = packed_stats(
                    [top[a : a + TB, :] for a in r], [acc[a : a + TB, HD : 2 * HD] for a in r]
                )
                held[half][block // 8] = jnp.where(lane == block % 8, st, held[half][block // 8])
    for half, out in enumerate((out0, out1)):
        for group in range(2):
            out[512:544, group * HD : (group + 1) * HD] = held[half][group].astype(jnp.bfloat16)


def own_part(owner, info, bufs, okv):
    return pl.pallas_call(
        own_kernel,
        out_shape=(PART,) * 2,
        in_specs=[SMEM, SMEM] + [HBM] * 5 + [VMEM],
        out_specs=(VMEM,) * 2,
        scratch_shapes=[
            pltpu.VMEM((4, 4, TB, 512), jnp.bfloat16),
            pltpu.SMEM((16,), jnp.int32),
            pltpu.SMEM((8,), jnp.int32),
            pltpu.SemaphoreType.DMA((16,)),
        ],
        compiler_params=pltpu.CompilerParams(vmem_limit_bytes=16 * 2**20),
        cost_estimate=pl.CostEstimate(
            flops=2 * 2 * 2048 * 256 * 256, bytes_accessed=4 * 2**20, transcendentals=2**19
        ),
        name="own_part",
    )(owner, info, *bufs, okv)


def combine_kernel(step, owner, lengths, info, *rest):
    parts, rest = rest[:5], rest[5:]
    if step > 0:
        first, rest = rest[0], rest[1:]
    out, body, tail, place, count, sem = rest
    x, core = info[1], info[2]
    group = (0, 1 - core, core)[step]
    size = 512 if step == 0 else 256
    rows = pl.ds(pl.multiple_of(group * 256, 256), size)
    columns = pl.ds(pl.multiple_of(group * HD, HD), size // 2)
    copies = []
    for i, part in enumerate(parts):
        copies.append(pltpu.make_async_copy(part.at[rows, :], body.at[i], sem.at[2 * i]))
        copies.append(
            pltpu.make_async_copy(part.at[512:544, columns], tail.at[i], sem.at[2 * i + 1])
        )
    for c in copies:
        c.start()
    rank(owner, place, count)
    lane = lax.broadcasted_iota(jnp.int32, (HD, 512), 0)
    col = lax.broadcasted_iota(jnp.int32, (HD, 512), 1)
    kind = (lane & 7) - 3 * (col >> 8)
    pick = (((lane >> 3) & 1) == ((col >> 7) & 1)) & (kind >= 0) & (kind < 3)
    pick = pick.astype(jnp.float32).astype(jnp.bfloat16)
    block = lax.broadcasted_iota(jnp.int32, (TB, HD), 1) >> 4
    row = lax.broadcasted_iota(jnp.int32, (128, 1), 0)
    token = (row >> 5) * (2 * TB) + core * TB + (row & (TB - 1))

    if step > 0:
        out[:, 0:256] = first[rows, :]
    for c in copies:
        c.wait()
    for slot in range(size // 128):
        valid = token < lengths[place[(x * 2 + group) * 2 + slot]]
        wide = []
        for i in range(5):
            st = tail[i, :, (slot // 2) * HD : (slot // 2 + 1) * HD].astype(jnp.float32)
            st = jnp.concatenate(
                [jnp.where(block == (slot % 2) * 4 + b, st, 0.0) for b in range(4)], axis=0
            )
            wide.append(
                lax.dot_general(
                    st.astype(jnp.bfloat16), pick, NN, preferred_element_type=jnp.float32
                )
            )
        top = functools.reduce(jnp.maximum, [w[:, 0:256] for w in wide])
        numer, denom = 0.0, 0.0
        for i, w in enumerate(wide):
            f = jnp.exp2(w[:, 0:256] - top)
            numer = numer + body[i, slot * 128 : (slot + 1) * 128, :].astype(jnp.float32) * f
            denom = denom + w[:, 256:512] * f
        done = jnp.where(valid, numer / denom, 0.0).astype(jnp.bfloat16)
        if step == 0:
            out[slot * 128 : (slot + 1) * 128, :] = done
        else:
            out[slot * 128 : (slot + 1) * 128, 256:512] = done


def combine(step, owner, lengths, info, parts, *more):
    size = 512 if step == 0 else 256
    shape = (512, 256) if step == 0 else (256, 512)
    return pl.pallas_call(
        functools.partial(combine_kernel, step),
        out_shape=jax.ShapeDtypeStruct(shape, jnp.bfloat16),
        in_specs=[SMEM, SMEM, SMEM] + [ANY] * 5 + [VMEM] * len(more),
        out_specs=VMEM,
        scratch_shapes=[
            pltpu.VMEM((5, size, 256), jnp.bfloat16),
            pltpu.VMEM((5, TB, size // 2), jnp.bfloat16),
            pltpu.SMEM((16,), jnp.int32),
            pltpu.SMEM((8,), jnp.int32),
            pltpu.SemaphoreType.DMA((10,)),
        ],
        compiler_params=pltpu.CompilerParams(vmem_limit_bytes=12 * 2**20),
        name=f"combine_{step}",
    )(owner, lengths, info, *parts, *more)


def weave_kernel(info, mine, got, out):
    core = info[2]
    for slot in range(2):
        for tb in range(4):
            rows = slice(slot * 128 + tb * TB, slot * 128 + (tb + 1) * TB)
            for of, value in ((core, mine), (1 - core, got)):
                to = pl.ds(pl.multiple_of(slot * 256 + tb * 64 + of * TB, TB), TB)
                out[to, :] = value[rows, :]


def weave(info, mine, got):
    return pl.pallas_call(
        weave_kernel,
        out_shape=jax.ShapeDtypeStruct((512, 512), jnp.bfloat16),
        in_specs=[SMEM, VMEM, VMEM],
        out_specs=VMEM,
        compiler_params=pltpu.CompilerParams(vmem_limit_bytes=12 * 2**20),
        name="weave",
    )(info, mine, got)


def split_kernel(info, owner, left, right, cand, lower, upper, okvsend, own, count, sem):
    head = pl.multiple_of(info[0] * HD, HD)
    copies = [
        pltpu.make_async_copy(left.at[0:8], lower, sem.at[0]),
        pltpu.make_async_copy(right.at[8:16], upper, sem.at[1]),
        pltpu.make_async_copy(cand.at[:, :, pl.ds(head, HD)], own.at[:, :, 0:HD], sem.at[2]),
        pltpu.make_async_copy(
            cand.at[:, :, pl.ds(pl.multiple_of(head + KVH * HD, HD), HD)],
            own.at[:, :, HD : 2 * HD],
            sem.at[3],
        ),
    ]
    for c in copies:
        c.start()
    for o in range(8):
        count[o] = 0
    for c in copies:
        c.wait()
    for i in range(16):
        o = owner[i]
        slot = (o & 1) * 2 + count[o]
        count[o] = count[o] + 1
        for s in range(4):

            @pl.when(slot == s)
            def _(i=i, s=s, x=o >> 1):
                for core in range(2):
                    okvsend[x * 2 + core, :, s * 256 : (s + 1) * 256] = own[i]


def split(info, owner, left, right, cand):
    return pl.pallas_call(
        split_kernel,
        out_shape=(jax.ShapeDtypeStruct((8, 32, 512), jnp.bfloat16),) * 2
        + (jax.ShapeDtypeStruct((8, 32, 1024), jnp.bfloat16),),
        in_specs=[SMEM, SMEM, ANY, ANY, ANY],
        out_specs=(VMEM,) * 3,
        scratch_shapes=[
            pltpu.VMEM((16, 32, 256), jnp.bfloat16),
            pltpu.SMEM((8,), jnp.int32),
            pltpu.SemaphoreType.DMA((4,)),
        ],
        compiler_params=pltpu.CompilerParams(vmem_limit_bytes=LIMIT),
        cost_estimate=pl.CostEstimate(
            flops=2 * 10**11, bytes_accessed=2**21, transcendentals=0
        ),
        name="split",
    )(info, owner, left, right, cand)


CORE = [(i, i ^ 1) for i in range(8)]


def along_x(shift):
    return [(i, (i + 2 * shift) % 8) for i in range(8)]


def local(queries, cand_kv, prefix_kv, lengths, owner):
    g = lax.axis_index("group")
    info = jnp.stack([lax.axis_index("prefix") // 2, g // 2, g % 2, g]).astype(jnp.int32)
    swap = lambda a: lax.ppermute(a, "group", CORE)
    left = lax.ppermute(queries, "group", along_x(1))
    right = lax.ppermute(queries, "group", along_x(3))
    kvsend = prep(info, prefix_kv)
    kv0 = lax.all_to_all(kvsend, "prefix", split_axis=0, concat_axis=0, tiled=True)
    lower, upper, okvsend = split(info, owner, left, right, cand_kv)
    lower = lax.ppermute(lower, "group", along_x(1))
    upper = lax.ppermute(upper, "group", along_x(3))
    kv0, lower, upper = lax.optimization_barrier((kv0, lower, upper))
    kv0 = kv0.reshape(2048, 256)
    kv1 = swap(kv0)
    bufs = [queries, left, right, lower, upper]
    okvsend, _ = lax.optimization_barrier((okvsend, kv0))
    okv = lax.all_to_all(okvsend, "group", split_axis=0, concat_axis=0, tiled=True)
    send = lambda outs: [lax.ppermute(o, "group", along_x(s + 1)) for s, o in enumerate(outs)]
    mine0, *sent = flash(0, owner, lengths, info, bufs, kv0, kv1)
    got0 = send(sent)
    mine1, *sent = flash(1, owner, lengths, info, bufs, kv0, kv1)
    got1 = send(sent)
    okv, _ = lax.optimization_barrier((okv, mine1))
    own0, own1 = own_part(owner, info, bufs, okv)
    first = combine(0, owner, lengths, info, [mine0, *got0, own0])
    first, *got1 = lax.optimization_barrier((first, *got1))
    parts = [mine1, *got1, own1]
    got = swap(combine(1, owner, lengths, info, parts, first))
    mine = combine(2, owner, lengths, info, parts, first)
    return weave(info, mine, got).reshape(2, 256, 512)


def solution(mesh):
    return jax.shard_map(
        local,
        mesh=mesh,
        in_specs=(P(None, "group", "prefix"), P(None, "group", None), P("prefix", None), P(), P()),
        out_specs=P("group", None, "prefix"),
        check_vma=False,
    )
```
